128 devices in a mesh: row: 8 (over z, x_hi), col: 16 (over y, x_lo, core).
Axes of the slice: x: 4 (x_hi: 2, x_lo: 2; x = x_hi * 2 + x_lo), y: 4, z: 4, core: 2. Of those that a mesh axis runs over, the one named last changes fastest.
Arguments:
- blocks: bfloat16 [8, 16, 32, 256, 256], P('row', 'col'), may hold values from 0 to 1
- block_rows: int32 [8, 16, 32], P('row', 'col'), may hold values from 0 to 7, as said below
- block_cols: int32 [8, 16, 32], P('row', 'col'), may hold values from 0 to 3
- counts: int32 [8, 16], P('row', 'col'), may hold values from 1 to 32, as said below
- sections: int32 [2], replicated, may hold values from 0 to 15, as said below
Outputs:
- inflated: bfloat16 [16384, 16384], P('row', 'col')
The draws below stay inside these ranges and needn't reach their ends.
Inputs may be any that keep to these rules, and one draw needn't show every extreme that they name: `block_rows`: the live slots of one device name distinct blocks of its tile. `counts`: some device holds exactly 32 live slots. The two sections differ.
All inputs are finite; a program needn't handle non-finite values.
Results may differ from the reference program's by a relative error of at most 0.001.
Values may be sent and summed in bfloat16 or wider, within the bound.
No kernel may reach another device: no remote copies, remote signals or barrier semaphores. Data moves between devices by JAX's collectives and lax.ppermute only.
A program may use at most 192 MiB of HBM per device.

```python
import jax
import jax.numpy as jnp
from jax import lax

B = 256
TC = 4
CAP = 32
WINDOW = 2
SECTIONS_ALL = 16
GRID_R = 8
GRID_C = 16
TR = 8
PANEL = 4
TRACKS = 16384


def slot_positions(key):
    keys = jax.random.split(key, GRID_R * GRID_C)
    chosen = jax.vmap(lambda single: jax.random.permutation(single, TR * TC)[:CAP])(keys)
    return chosen.reshape(GRID_R, GRID_C, CAP).astype(jnp.int32)


def draw_block_rows(key, part):
    positions = slot_positions(key)
    return (positions // TC).astype(jnp.int32)


def draw_block_cols(key, part):
    positions = slot_positions(key)
    return (positions % TC).astype(jnp.int32)


def draw_counts(key, part):
    key = jax.random.fold_in(key, 13)
    first, second = jax.random.split(key)
    lowest = max(1, CAP // 6)
    values = jax.random.randint(first, (GRID_R * GRID_C,), lowest, CAP // 2 + 1).astype(jnp.int32)
    busiest = jax.random.randint(second, (), 0, GRID_R * GRID_C)
    values = values.at[busiest].set(CAP)
    return values.reshape(GRID_R, GRID_C).astype(jnp.int32)


def draw_sections(key, part):
    key = jax.random.fold_in(key, 14)
    first, second = jax.random.split(key)
    other = jax.random.randint(first, (), 0, SECTIONS_ALL - 1).astype(jnp.int32)
    last = jnp.int32(SECTIONS_ALL - 1)
    flip = jax.random.randint(second, (), 0, 2).astype(jnp.int32)
    leading = jnp.where(flip == 1, last, other)
    trailing = jnp.where(flip == 1, other, last)
    return jnp.stack([leading, trailing]).astype(jnp.int32)


def levels(stream_key, shape, cuts, least, top_value):
    def one(position, shards_of):
        steps = jax.random.uniform(jax.random.fold_in(jax.random.fold_in(stream_key, 6), position), (shards_of,), jnp.float32, least / len(cuts), top_value / len(cuts))
        return jnp.repeat(jnp.exp(steps), shape[position] // shards_of).reshape((-1,) + (1,) * (len(shape) - position - 1))

    loudness = one(*cuts[0])
    for cut in cuts[1:]:
        loudness = loudness * one(*cut)
    return loudness


def setup_inputs(seed: int = 0) -> dict:
    splits = jax.random.split(jax.random.key(seed), 6)
    blocks = jnp.clip(1.0 * jax.random.uniform(splits[0], (GRID_R, GRID_C, CAP, B, B), jnp.float32) ** levels(splits[0], (GRID_R, GRID_C, CAP, B, B), ((0, 8), (1, 16)), -0.2, 0.2), 0.0, 1.0).astype(jnp.bfloat16)
    block_rows = draw_block_rows(jax.random.fold_in(splits[5], 71), 0)
    block_cols = draw_block_cols(jax.random.fold_in(splits[5], 71), 0)
    counts = draw_counts(jax.random.fold_in(splits[5], 71), 0)
    sections = draw_sections(jax.random.fold_in(splits[5], 71), 0)
    return {"blocks": blocks, "block_rows": block_rows, "block_cols": block_cols, "counts": counts, "sections": sections}


EPS = 1e-6


def slot_places(rows, cols, count):
    slot = jnp.arange(rows.shape[-1], dtype=jnp.int32)
    return jnp.where(slot < count[..., None], rows * TC + cols, -1).astype(jnp.int32)


def build_strip(values, places, owner, section):
    local_row = places // TC
    local_col = places % TC
    index = owner * TR + local_row - section * PANEL
    usable = (places >= 0) & (index >= 0) & (index < PANEL)
    target = jnp.where(usable, index * TC + local_col, -1)
    onehot = (target[:, None] == jnp.arange(PANEL * TC, dtype=jnp.int32)[None, :]).astype(jnp.float32)
    flat = jnp.dot(onehot.T, values.astype(jnp.float32).reshape(values.shape[0], B * B), precision=lax.Precision.HIGHEST)
    strip = flat.reshape(PANEL, TC, B, B).transpose(0, 2, 1, 3).reshape(PANEL, B, TC * B)
    return strip.astype(jnp.bfloat16)


def multiply(accum, values, places, owner, strip, section):
    local_row = places // TC
    local_col = places % TC
    index = owner * TC + local_col - section * PANEL
    usable = (places >= 0) & (index >= 0) & (index < PANEL)
    picked = strip[jnp.clip(index, 0, PANEL - 1)]
    product = jnp.einsum("pab,pbn->pan", values.astype(jnp.float32), picked.astype(jnp.float32), precision=lax.Precision.HIGHEST)
    select = ((local_row[:, None] == jnp.arange(TR, dtype=jnp.int32)[None, :]) & usable[:, None]).astype(jnp.float32)
    return accum + jnp.einsum("pr,pan->ran", select, product, precision=lax.Precision.HIGHEST)


def reference(blocks, block_rows, block_cols, counts, sections):
    places = slot_places(block_rows, block_cols, counts)

    def tile(grid_row, grid_col):
        accum = jnp.zeros((TR, B, TC * B), jnp.float32)
        for window_step in range(WINDOW):
            section = sections[window_step]
            col_owner = (section * PANEL) // TC
            row_owner = (section * PANEL) // TR
            strip = build_strip(blocks[row_owner, grid_col], places[row_owner, grid_col], row_owner, section)
            accum = multiply(accum, blocks[grid_row, col_owner], places[grid_row, col_owner], col_owner, strip, section)
        return accum * accum

    def column(grid_col):
        squared = lax.map(lambda grid_row: tile(grid_row, grid_col), jnp.arange(GRID_R, dtype=jnp.int32))
        total = jnp.sum(squared, axis=(0, 1, 2))
        return (TRACKS * squared / (total + EPS)).astype(jnp.bfloat16)

    result = lax.map(column, jnp.arange(GRID_C, dtype=jnp.int32))
    return result.transpose(1, 2, 3, 0, 4).reshape(TRACKS, TRACKS)
```

```python
import functools

import jax
import jax.numpy as jnp
from jax import lax
from jax.experimental import pallas as pl
from jax.experimental.pallas import tpu as pltpu
from jax.sharding import PartitionSpec as P

B = 256
TC = 4
TR = 8
CAP = 32
WINDOW = 2
SECTIONS_ALL = 16
PANEL = 4
EPS = 1e-06

KC = 16
KR = 12
CS = KC // 8
RS = KR // 4
HEAD = 16
C_ROWS = CS * B + HEAD
R_ROWS = RS * B + HEAD
TOTAL_ROW = 8

ANY = pl.BlockSpec(memory_space=pl.ANY)
SMEM = pl.BlockSpec(memory_space=pltpu.SMEM)


def from_root(block, axis, holder):
    block = jnp.where(lax.axis_index(axis) == holder, block, jnp.zeros_like(block))
    return lax.psum(block, axis)


def build_strip(values, places, owner, section, panel, tile_rows):
    local_row = places // TC
    local_col = places % TC
    index = owner * tile_rows + local_row - section * panel
    usable = (places >= 0) & (index >= 0) & (index < panel)
    target = jnp.where(usable, index * TC + local_col, -1)
    onehot = (target[:, None] == jnp.arange(panel * TC, dtype=jnp.int32)[None, :]).astype(
        jnp.bfloat16
    )
    flat = lax.dot_general(
        onehot,
        values.reshape(values.shape[0], B * B),
        (((0,), (0,)), ((), ())),
        preferred_element_type=jnp.float32,
    )
    strip = flat.reshape(panel, TC, B, B).transpose(0, 2, 1, 3).reshape(panel, B, TC * B)
    return strip.astype(jnp.bfloat16)


def multiply(accum, values, places, owner, strip, section, panel, tile_rows):
    local_row = places // TC
    local_col = places % TC
    index = owner * TC + local_col - section * panel
    usable = (places >= 0) & (index >= 0) & (index < panel)
    picked = strip[jnp.clip(index, 0, panel - 1)]
    product = jnp.einsum("pab,pbn->pan", values, picked, preferred_element_type=jnp.float32)
    select = (
        (local_row[:, None] == jnp.arange(tile_rows, dtype=jnp.int32)[None, :]) & usable[:, None]
    ).astype(jnp.float32)
    return accum + jnp.einsum("pr,pan->ran", select, product, precision=lax.Precision.HIGHEST)


def one_chip(values, rows, cols, count, sections):
    slot = jnp.arange(values.shape[0], dtype=jnp.int32)
    places = jnp.where(slot < count, rows * TC + cols, -1)
    my_row = lax.axis_index("row")
    accum = jnp.zeros((TR, B, TC * B), jnp.float32)
    for step in range(WINDOW):
        section = sections[step]
        col_owner = section * PANEL // TC
        row_owner = section * PANEL // TR
        col_values = from_root(values, "col", col_owner)
        col_places = from_root(places, "col", col_owner)
        own_strip = build_strip(values, places, my_row, section, PANEL, TR)
        strip = from_root(own_strip, "row", row_owner)
        accum = multiply(accum, col_values, col_places, col_owner, strip, section, PANEL, TR)
    squared = accum * accum
    total = lax.psum(jnp.sum(squared, axis=(0, 1)), "row")
    scaled = TR * 8 * B * squared / (total + EPS)
    return scaled.reshape(TR * B, TC * B).astype(jnp.bfloat16)


def head_tile(values):
    row = lax.broadcasted_iota(jnp.int32, (HEAD, B), 0)
    tile = jnp.zeros((HEAD, B), jnp.int32)
    for m, value in values:
        tile = jnp.where(row == m, value, tile)
    return tile.astype(jnp.float32).astype(jnp.bfloat16)


def pack_c_kernel(offset, info, rows, cols, values, mine, other, heads, sems):
    i, j, t0, t1, count = info[0], info[1], info[2], info[3], info[4]

    @pl.when((j == t0) | (j == t1))
    def _():
        core = lax.rem(j, 2)
        copies = []
        for side, out in enumerate((mine, other)):
            lane = core if side == 0 else 1 - core
            for p in range(4):
                slot = offset + lane * (KC // 2) + p * CS
                n = side * 4 + p
                copies.append(
                    pltpu.make_async_copy(
                        values.at[pl.ds(pl.multiple_of(slot * B, B), CS * B)],
                        out.at[p, pl.ds(0, CS * B)],
                        sems.at[n],
                    )
                )
                copies[-1].start()
                entries = []
                for m in range(CS):
                    at = slot + m
                    place = rows[at] * TC + cols[at] + 1
                    entries.append((m, jnp.where(at < count, place, 0)))
                entries.append((TOTAL_ROW, count))
                heads[n] = head_tile(entries)
                copies.append(
                    pltpu.make_async_copy(
                        heads.at[n], out.at[p, pl.ds(CS * B, HEAD)], sems.at[8 + n]
                    )
                )
                copies[-1].start()
        for copy in copies:
            copy.wait()


def pack_c(offset, info, rows, cols, values):
    out = jax.ShapeDtypeStruct((4, C_ROWS, B), jnp.bfloat16)
    return pl.pallas_call(
        functools.partial(pack_c_kernel, offset),
        out_shape=(out, out),
        in_specs=[SMEM, SMEM, SMEM, ANY],
        out_specs=(ANY, ANY),
        scratch_shapes=[pltpu.VMEM((8, HEAD, B), jnp.bfloat16), pltpu.SemaphoreType.DMA((16,))],
        name="pack_c",
    )(info, rows, cols, values)


def pack_r_kernel(offset, info, rows, cols, values, out, place, heads, sems, head_sems):
    i, j, t0, t1, count = info[0], info[1], info[2], info[3], info[4]
    first = i == t0 // 2

    @pl.when(first | (i == t1 // 2))
    def _():
        half = lax.rem(jnp.where(first, t0, t1), 2)
        for k in range(KR):
            place[k] = 0

        def copy(slot, k):
            return pltpu.make_async_copy(
                values.at[pl.ds(pl.multiple_of(slot * B, B), B)],
                out.at[k // RS, pl.ds(pl.multiple_of(lax.rem(k, RS) * B, B), B)],
                sems.at[k],
            )

        def step(slot, seen):
            live = rows[slot] // PANEL == half
            k = seen - offset

            @pl.when(live & (k >= 0) & (k < KR))
            def _():
                place[k] = lax.rem(rows[slot], PANEL) * TC + cols[slot] + 1
                copy(slot, k).start()

            return seen + live.astype(jnp.int32)

        seen = lax.fori_loop(0, count, step, jnp.int32(0))
        for p in range(4):
            entries = [(m, place[p * RS + m]) for m in range(RS)]
            entries.append((TOTAL_ROW, seen))
            heads[p] = head_tile(entries)
        head_copies = [
            pltpu.make_async_copy(heads.at[p], out.at[p, pl.ds(RS * B, HEAD)], head_sems.at[p])
            for p in range(4)
        ]
        for c in head_copies:
            c.start()
        for c in head_copies:
            c.wait()

        def finish(k, carry):
            copy(0, k).wait()
            return carry

        lax.fori_loop(0, jnp.clip(seen - offset, 0, KR), finish, 0)


def pack_r(offset, info, rows, cols, values):
    return pl.pallas_call(
        functools.partial(pack_r_kernel, offset),
        out_shape=jax.ShapeDtypeStruct((4, R_ROWS, B), jnp.bfloat16),
        in_specs=[SMEM, SMEM, SMEM, ANY],
        out_specs=ANY,
        scratch_shapes=[
            pltpu.SMEM((KR,), jnp.int32),
            pltpu.VMEM((4, HEAD, B), jnp.bfloat16),
            pltpu.SemaphoreType.DMA((KR,)),
            pltpu.SemaphoreType.DMA((4,)),
        ],
        name="pack_r",
    )(info, rows, cols, values)


def unwritten(shapes):
    return pl.pallas_call(
        lambda *refs: None,
        out_shape=tuple(jax.ShapeDtypeStruct(s, jnp.bfloat16) for s in shapes),
        out_specs=tuple(ANY for _ in shapes),
        name="unwritten",
    )()


class Ring:
    def __init__(self, axis, size, step, swap):
        self.axis, self.size, self.step, self.swap = axis, size, step, swap

    def shift(self, x, by):
        n = self.size
        return lax.ppermute(x, self.axis, [(a, (a + by * self.step) % n) for a in range(n)])

    def cross(self, x):
        return lax.ppermute(x, self.axis, [(a, a ^ self.swap) for a in range(self.size)])

    def others(self, x):
        return [self.shift(x, 1), self.shift(x, -1), self.shift(x, 2)]


COL = Ring("col", 16, 4, 2)
ROW = Ring("row", 8, 2, 1)


def spread(ring, piece_of, t0, t1, position, plane, shapes):
    own = piece_of(position)
    ahead = ring.shift(piece_of((position + 1) % 4), 1)
    back = ring.shift(piece_of((position + 3) % 4), -1)
    far = ring.shift(piece_of((position + 2) % 4), 2)

    def quarter(t):
        away = (position - t // 4 + 4) % 4
        return jnp.where(
            away == 0, own, jnp.where(away == 1, ahead, jnp.where(away == 2, far, back))
        )

    plane0, plane1 = (t0 // 2) % 2, (t1 // 2) % 2
    same = plane0 == plane1
    at0 = plane == plane0
    first = quarter(jnp.where(at0, t0, t1))
    crossed = ring.cross(first)
    round_a = [first] + ring.others(first)
    second = jnp.where(same & at0, quarter(t1), crossed)
    round_b = [second] + ring.others(second)

    def more(x):
        x = ring.cross(x)
        return tuple([x] + ring.others(x))

    round_c = lax.cond(same, more, lambda x: unwritten([x.shape] * 4), second)
    section_a = jnp.where(at0, 0, jnp.where(same, -1, 1))
    section_b = jnp.where(at0, 1, 0)
    section_c = jnp.where(same & ~at0, 1, -1)
    return (round_a, round_b, list(round_c)), (section_a, section_b, section_c)


def send_c(offset, info, rows, cols, values):
    j, t0, t1 = info[1], info[2], info[3]
    core = j % 2
    mine, other = pack_c(offset, info, rows, cols, values)
    swap = [(a, a ^ 1) for a in range(16)]
    got = lax.ppermute(other, "col", swap)
    t = jnp.where(j // 2 == t0 // 2, t0, t1)
    keep = core == t % 2

    def piece_of(p):
        return jnp.where(
            keep,
            lax.dynamic_index_in_dim(mine, p, 0, False),
            lax.dynamic_index_in_dim(got, p, 0, False),
        )

    rounds, sections = spread(COL, piece_of, t0, t1, j // 4, (j // 2) % 2, None)
    out = []
    for n, pieces in enumerate(rounds):
        lane = jnp.stack(pieces)
        if n < 2:
            out.append((lane, lax.ppermute(lane, "col", swap)))
        else:
            same = (t0 // 2) % 2 == (t1 // 2) % 2
            out.append(
                (
                    lane,
                    lax.cond(
                        same,
                        lambda x: lax.ppermute(x, "col", swap),
                        lambda x: unwritten([x.shape])[0],
                        lane,
                    ),
                )
            )
    return [a for pair in out for a in pair], jnp.stack(sections)


def send_r(offset, info, rows, cols, values):
    i, t0, t1 = info[0], info[2], info[3]
    packed = pack_r(offset, info, rows, cols, values)

    def piece_of(p):
        return lax.dynamic_index_in_dim(packed, p, 0, False)

    rounds, sections = spread(ROW, piece_of, t0, t1, i // 2, i % 2, None)
    return [a for pieces in rounds for a in pieces], jnp.stack(sections)


def c_heads(arrays):
    return jnp.stack([a[:, CS * B :, 0] for a in arrays]).astype(jnp.int32)


def r_heads(arrays):
    return jnp.stack([a[RS * B :, 0] for a in arrays]).astype(jnp.int32)


def product_kernel(
    c_sections, r_sections, c_head, r_head, *refs
):
    rounds = 2
    c_refs, refs = refs[: 6 * rounds], refs[6 * rounds :]
    r_refs, refs = refs[: 12 * rounds], refs[12 * rounds :]
    out, sums, accum, left, right, at_row, at_k, there, counter, c_sem, r_sem, o_sem = refs
    for n in range(WINDOW * PANEL * TC):
        there[n] = 0
    counter[0] = 0
    counter[1] = 0

    def from_any(dst, sem):
        return pltpu.make_async_copy(c_refs[0].at[0, pl.ds(0, B)], dst, sem)

    for r in range(rounds):
        for n in range(12):
            section = r_sections[r * 3 + n // 4]

            @pl.when(section >= 0)
            def _():
                for m in range(RS):
                    place = r_head[r * 12 + n, m] - 1

                    @pl.when(place >= 0)
                    def _():
                        at = section * (PANEL * TC) + place
                        there[at] = 1
                        count = counter[1]
                        pltpu.make_async_copy(
                            r_refs[r * 12 + n].at[pl.ds(m * B, B)],
                            right.at[at],
                            r_sem.at[count],
                        ).start()
                        counter[1] = count + 1

        for n in range(6):
            section = c_sections[r * 3 + n // 2]

            @pl.when(section >= 0)
            def _():
                for p in range(4):
                    for m in range(CS):
                        place = c_head[(r * 6 + n) * 4 + p, m] - 1

                        @pl.when(place >= 0)
                        def _():
                            count = counter[0]
                            at_row[count] = place // TC
                            at_k[count] = section * PANEL + lax.rem(place, TC)
                            pltpu.make_async_copy(
                                c_refs[r * 6 + n].at[p, pl.ds(m * B, B)],
                                left.at[count],
                                c_sem.at[count],
                            ).start()
                            counter[0] = count + 1

    @pl.loop(0, TR)
    def _(r):
        accum[pl.ds(pl.multiple_of(r * B, B), B), :] = jnp.zeros((B, TC * B), jnp.float32)

    @pl.loop(0, counter[1])
    def _(n):
        from_any(right.at[0], r_sem.at[n]).wait()

    @pl.loop(0, counter[0])
    def _(n):
        from_any(left.at[0], c_sem.at[n]).wait()
        at = pl.ds(pl.multiple_of(at_row[n] * B, B), B)
        k = at_k[n]
        for c in range(TC):

            @pl.when(there[k * TC + c] > 0)
            def _():
                accum[at, c * B : (c + 1) * B] += jnp.dot(
                    left[n], right[k * TC + c], preferred_element_type=jnp.float32
                )

    total = jnp.zeros((8, TC * B), jnp.float32)
    copies = []
    for r in range(TR):
        copies.append(
            pltpu.make_async_copy(
                accum.at[pl.ds(r * B, B)], out.at[pl.ds(r * B, B)], o_sem.at[r]
            )
        )
        copies[-1].start()

        def add(s, total, r=r):
            x = accum[pl.ds(pl.multiple_of(r * B + s * 8, 8), 8), :]
            return total + x * x

        total = lax.fori_loop(0, B // 8, add, total)
    sums[...] = jnp.sum(total, axis=0, keepdims=True)
    for copy in copies:
        copy.wait()


def products(c_sections, r_sections, c_head, r_head, c_arrays, r_arrays):
    slots = WINDOW * CAP
    blocks = WINDOW * PANEL * TC
    return pl.pallas_call(
        product_kernel,
        out_shape=(
            jax.ShapeDtypeStruct((TR * B, TC * B), jnp.float32),
            jax.ShapeDtypeStruct((1, TC * B), jnp.float32),
        ),
        in_specs=[SMEM] * 4 + [ANY] * (len(c_arrays) + len(r_arrays)),
        out_specs=(ANY, pl.BlockSpec(memory_space=pltpu.VMEM)),
        scratch_shapes=[
            pltpu.VMEM((TR * B, TC * B), jnp.float32),
            pltpu.VMEM((slots, B, B), jnp.bfloat16),
            pltpu.VMEM((blocks, B, B), jnp.bfloat16),
            pltpu.SMEM((slots,), jnp.int32),
            pltpu.SMEM((slots,), jnp.int32),
            pltpu.SMEM((blocks,), jnp.int32),
            pltpu.SMEM((2,), jnp.int32),
            pltpu.SemaphoreType.DMA((slots,)),
            pltpu.SemaphoreType.DMA((blocks,)),
            pltpu.SemaphoreType.DMA((TR,)),
        ],
        compiler_params=pltpu.CompilerParams(vmem_limit_bytes=40 * 1024 * 1024),
        name="products",
    )(c_sections, r_sections, c_head, r_head, *c_arrays, *r_arrays)


def scale_kernel(total, x, out):
    value = x[...]
    factor = (TR * 8 * B) / (total[...] + EPS)
    out[...] = (value * value * factor).astype(jnp.bfloat16)


def scale(total, expanded):
    return pl.pallas_call(
        scale_kernel,
        grid=(TR,),
        out_shape=jax.ShapeDtypeStruct((TR * B, TC * B), jnp.bfloat16),
        in_specs=[
            pl.BlockSpec((1, TC * B), lambda r: (0, 0)),
            pl.BlockSpec((B, TC * B), lambda r: (r, 0)),
        ],
        out_specs=pl.BlockSpec((B, TC * B), lambda r: (r, 0)),
        name="scale",
    )(total, expanded)


def column_total(part):
    part = part + sum([ROW.shift(part, by) for by in (1, 2, 3)])
    return part + ROW.cross(part)


def two_chips(values, rows, cols, count, sections):
    flat = values.reshape(CAP * B, B)
    info = jnp.stack(
        [lax.axis_index("row"), lax.axis_index("col"), sections[0], sections[1], count]
    ).astype(jnp.int32)
    args = (info, rows, cols, flat)
    r_arrays, r_sections = send_r(0, *args)
    c_arrays, c_sections = send_c(0, *args)
    r_head = r_heads(r_arrays)
    c_head = c_heads(c_arrays)
    r_over = jnp.any((r_sections >= 0) & (r_head[::4, TOTAL_ROW] > KR))
    c_over = jnp.any((c_sections >= 0) & (c_head[::2, 0, TOTAL_ROW] > KC))

    def again(send):
        def run(*args):
            arrays, sections = send(*args)
            return tuple(arrays), sections

        return run

    def nothing(shapes):
        return lambda *args: (unwritten(shapes), jnp.full((3,), -1, jnp.int32))

    r_more, r_more_sections = lax.cond(
        r_over,
        again(functools.partial(send_r, KR)),
        nothing([a.shape for a in r_arrays]),
        *args,
    )
    c_more, c_more_sections = lax.cond(
        c_over,
        again(functools.partial(send_c, KC)),
        nothing([a.shape for a in c_arrays]),
        *args,
    )
    expanded, part = products(
        jnp.concatenate([c_sections, c_more_sections]),
        jnp.concatenate([r_sections, r_more_sections]),
        jnp.concatenate([c_head, c_heads(c_more)]).reshape(-1, HEAD),
        jnp.concatenate([r_head, r_heads(r_more)]),
        list(c_arrays) + list(c_more),
        list(r_arrays) + list(r_more),
    )
    return scale(column_total(part), expanded)


def per_device(blocks, block_rows, block_cols, counts, sections):
    return lax.cond(
        sections[0] // 2 == sections[1] // 2,
        one_chip,
        two_chips,
        blocks[0, 0],
        block_rows[0, 0],
        block_cols[0, 0],
        counts[0, 0],
        sections,
    )


def solution(mesh):
    in_specs = (
        P("row", "col", None, None, None),
        P("row", "col", None),
        P("row", "col", None),
        P("row", "col"),
        P(),
    )
    out_specs = P("row", "col")
    return jax.shard_map(
        per_device, mesh=mesh, in_specs=in_specs, out_specs=out_specs, check_vma=False
    )
```

```python
import functools

import jax
import jax.numpy as jnp
from jax import lax
from jax.experimental import pallas as pl
from jax.experimental.pallas import tpu as pltpu
from jax.sharding import PartitionSpec as P

B = 256
TC = 4
TR = 8
CAP = 32
WINDOW = 2
SECTIONS_ALL = 16
PANEL = 4
EPS = 1e-06

PS = 5
SLOTS = 4 * PS
HEAD = 16
ROWS = PS * B + HEAD
TOTAL = 100

ANY = pl.BlockSpec(memory_space=pl.ANY)
VMEM = pl.BlockSpec(memory_space=pltpu.VMEM)
SMEM = pl.BlockSpec(memory_space=pltpu.SMEM)
HBM = pl.BlockSpec(memory_space=pltpu.HBM)


def head_tile(values):
    lane = lax.broadcasted_iota(jnp.int32, (HEAD, B), 1)
    tile = jnp.zeros((HEAD, B), jnp.int32)
    for m, value in values:
        tile = jnp.where(lane == m, value, tile)
    return tile.astype(jnp.float32).astype(jnp.bfloat16)


def blocks_at(n):
    return pl.ds(pl.multiple_of(n * B, B), B)


def my_half(which, i, t0, t1):
    first = (i == t0 // 2) & (which == 0)
    return lax.rem(jnp.where(first, t0, t1), 2)


def c_code(rows, cols, slot):
    return rows[slot] * TC + cols[slot] + 1


def r_code(rows, cols, slot, core):
    return lax.rem(rows[slot], PANEL) * TC + cols[slot] + 1 + core * PANEL * TC


def pack_kernel(offset, which, info, rows, cols, values, out, place, sems):
    i, j, t0, t1, count = info[0], info[1], info[2], info[3], info[4]
    core = lax.rem(j, 2)

    def copy(slot, k):
        return pltpu.make_async_copy(
            values.at[blocks_at(slot)], out.at[blocks_at(k)], sems.at[k]
        )

    def finish(n, total):
        entries = [(k, place[k]) for k in range(SLOTS)] + [(TOTAL, total)]
        out[SLOTS * B :, :] = head_tile(entries)

        @pl.loop(0, n)
        def _(k):
            copy(0, k).wait()

    @pl.when((core == 1) & ((j == t0) | (j == t1)))
    def _():
        for k in range(SLOTS):
            place[k] = 0
        n = jnp.clip(count - offset, 0, SLOTS)

        @pl.loop(0, n)
        def _(k):
            place[k] = c_code(rows, cols, offset + k)
            copy(offset + k, k).start()

        finish(n, count)

    @pl.when((core == 0) & ((i == t0 // 2) | (i == t1 // 2)))
    def _():
        for k in range(SLOTS):
            place[k] = 0
        half = my_half(which, i, t0, t1)

        def step(slot, seen):
            live = rows[slot] // PANEL == half

            @pl.when(live)
            def _():
                place[seen] = r_code(rows, cols, slot, 0)
                copy(slot, seen).start()

            return seen + live.astype(jnp.int32)

        n = lax.fori_loop(0, count, step, jnp.int32(0))
        finish(n, n)


def pack(offset, which, info, rows, cols, values):
    return pl.pallas_call(
        functools.partial(pack_kernel, offset, which),
        out_shape=jax.ShapeDtypeStruct((SLOTS * B + HEAD, B), jnp.bfloat16),
        in_specs=[SMEM, SMEM, SMEM, ANY],
        out_specs=VMEM,
        scratch_shapes=[pltpu.SMEM((SLOTS,), jnp.int32), pltpu.SemaphoreType.DMA((SLOTS,))],
        name="pack",
    )(info, rows, cols, values)


def arrange_kernel(offset, which, info, rows, cols, values, got, *refs):
    outs, (place, tile, wide, heads, sems, head_sem) = refs[:4], refs[4:]
    i, j, t0, t1, count = info[0], info[1], info[2], info[3], info[4]
    core = lax.rem(j, 2)
    position = jnp.where(core == 0, j // 4, i // 2)
    c_root = (core == 0) & ((j // 2 == t0 // 2) | (j // 2 == t1 // 2))
    r_root = (core == 1) & ((i == t0 // 2) | (i == t1 // 2))

    def start(src, q):
        away = lax.rem(q // PS - position + 4, 4)
        for by in range(4):

            @pl.when(away == by)
            def _():
                pltpu.make_async_copy(
                    src, outs[by].at[blocks_at(lax.rem(q, PS))], sems.at[q]
                ).start()

    def finish(n, total):
        for by in range(4):
            p = lax.rem(position + by, 4)
            entries = [(m, place[p * PS + m]) for m in range(PS)] + [(TOTAL, total)]
            outs[by][PS * B :, :] = head_tile(entries)

        @pl.loop(0, n)
        def _(q):
            pltpu.make_async_copy(
                values.at[pl.ds(0, B)], outs[0].at[pl.ds(0, B)], sems.at[q]
            ).wait()

    @pl.when(c_root | r_root)
    def _():
        for q in range(SLOTS):
            place[q] = 0
        copy = pltpu.make_async_copy(got.at[pl.ds(SLOTS * B, HEAD)], tile, head_sem)
        copy.start()
        copy.wait()
        wide[...] = tile[:8, :128].astype(jnp.float32).astype(jnp.int32)
        copy = pltpu.make_async_copy(wide, heads, head_sem)
        copy.start()
        copy.wait()

    @pl.when(c_root)
    def _():
        first = (j // 2 == t0 // 2) & (which == 0)
        own = lax.rem(jnp.where(first, t0, t1), 2) == 0
        total = jnp.where(own, count, heads[0, TOTAL])
        n = jnp.clip(total - offset, 0, SLOTS)

        @pl.loop(0, n)
        def _(q):
            @pl.when(own)
            def _():
                place[q] = c_code(rows, cols, offset + q)
                start(values.at[blocks_at(offset + q)], q)

            @pl.when(jnp.logical_not(own))
            def _():
                place[q] = heads[0, q]
                start(got.at[blocks_at(q)], q)

        finish(n, total)

    @pl.when(r_root)
    def _():
        half = my_half(which, i, t0, t1)
        other = heads[0, TOTAL]

        @pl.loop(0, other)
        def _(k):
            q = k - offset

            @pl.when((q >= 0) & (q < SLOTS))
            def _():
                place[q] = heads[0, k]
                start(got.at[blocks_at(k)], q)

        def step(slot, seen):
            live = rows[slot] // PANEL == half
            q = seen - offset

            @pl.when(live & (q >= 0) & (q < SLOTS))
            def _():
                place[q] = r_code(rows, cols, slot, 1)
                start(values.at[blocks_at(slot)], q)

            return seen + live.astype(jnp.int32)

        total = lax.fori_loop(0, count, step, other)
        finish(jnp.clip(total - offset, 0, SLOTS), total)


def arrange(offset, which, info, rows, cols, values, got):
    own, ahead, far, back = pl.pallas_call(
        functools.partial(arrange_kernel, offset, which),
        out_shape=(jax.ShapeDtypeStruct((ROWS, B), jnp.bfloat16),) * 4,
        in_specs=[SMEM, SMEM, SMEM, ANY, ANY],
        out_specs=(VMEM,) * 4,
        scratch_shapes=[
            pltpu.SMEM((SLOTS,), jnp.int32),
            pltpu.VMEM((HEAD, B), jnp.bfloat16),
            pltpu.VMEM((8, 128), jnp.int32),
            pltpu.SMEM((8, 128), jnp.int32),
            pltpu.SemaphoreType.DMA((SLOTS,)),
            pltpu.SemaphoreType.DMA,
        ],
        name="arrange",
    )(info, rows, cols, values, got)
    return own, ahead, back, far


def unwritten(count, shape):
    return pl.pallas_call(
        lambda *refs: None,
        out_shape=(jax.ShapeDtypeStruct(shape, jnp.bfloat16),) * count,
        out_specs=(ANY,) * count,
        name="unwritten",
    )()


GRID_R, GRID_C = 8, 16


def permute(x, to_c, to_r, lanes):
    pairs = []
    for i in range(GRID_R):
        for j in range(GRID_C):
            if j % 2 == 0 and "c" in lanes:
                pairs.append((i * GRID_C + j, i * GRID_C + to_c(j) % GRID_C))
            if j % 2 == 1 and "r" in lanes:
                pairs.append((i * GRID_C + j, to_r(i) % GRID_R * GRID_C + j))
    return lax.ppermute(x, ("row", "col"), pairs)


def shift(x, by, lanes):
    return permute(x, lambda j: j + 4 * by, lambda i: i + 2 * by, lanes)


def cross(x, lanes):
    return permute(x, lambda j: j ^ 2, lambda i: i ^ 1, lanes)


def swap_cores(x):
    return lax.ppermute(x, "col", [(a, a ^ 1) for a in range(GRID_C)])


def others(x, lanes):
    return [shift(x, 1, lanes), shift(x, -1, lanes), shift(x, 2, lanes)]


def send(offset, lanes, info, rows, cols, values):
    i, j, t0, t1 = info[0], info[1], info[2], info[3]
    core = j % 2
    position = jnp.where(core == 0, j // 4, i // 2)
    one_root = t0 // 2 == t1 // 2
    plane0 = (t0 // 2) % 2
    same = plane0 == (t1 // 2) % 2
    c_at0, r_at0 = (j // 2) % 2 == plane0, i % 2 == plane0
    at0 = jnp.where(core == 0, c_at0, r_at0)

    def scatter(which):
        got = swap_cores(pack(offset, which, info, rows, cols, values))
        own, ahead, back, far = arrange(offset, which, info, rows, cols, values, got)
        ahead, back, far = shift(ahead, 1, lanes), shift(back, -1, lanes), shift(far, 2, lanes)

        def quarter(t):
            away = (position - t // 4 + 4) % 4
            return jnp.where(
                away == 0, own, jnp.where(away == 1, ahead, jnp.where(away == 2, far, back))
            )

        return quarter

    def step(x, far=None):
        pieces, far = lax.optimization_barrier((others(x, lanes), far(x, lanes) if far else ()))
        pieces = [x] + pieces
        return pieces + [swap_cores(p) for p in pieces], far

    quarter = scatter(0)
    first = quarter(jnp.where(at0, t0, t1))
    extra = lax.cond(
        one_root, lambda: scatter(1)(t1), lambda: unwritten(1, (ROWS, B))[0]
    )
    step_a, crossed = step(first, cross)
    second = jnp.where(
        same & at0, jnp.where(one_root, extra, quarter(t1)), crossed
    )
    step_b, crossed = step(second, cross)
    step_c = lax.cond(
        same,
        lambda x: tuple(step(x)[0]),
        lambda x: unwritten(8, (ROWS, B)),
        crossed,
    )

    def sections(at0):
        return [
            jnp.where(at0, 0, jnp.where(same, -1, 1)),
            jnp.where(at0, 1, 0),
            jnp.where(same & ~at0, 1, -1),
        ]

    c_sections = sections(c_at0) if "c" in lanes else [-1] * 3
    r_sections = sections(r_at0) if "r" in lanes else [-1] * 3
    where_to = jnp.stack([jnp.asarray(x, jnp.int32) for x in c_sections + r_sections])
    return tuple(step_a) + tuple(step_b) + tuple(step_c), where_to


def overflow_kernel(sections, *refs):
    arrays, (out, tiles, sems) = refs[:6], refs[6:]
    copies = [
        pltpu.make_async_copy(a.at[pl.ds(PS * B, HEAD)], tiles.at[n], sems.at[n])
        for n, a in enumerate(arrays)
    ]
    for copy in copies:
        copy.start()
    for copy in copies:
        copy.wait()
    x = jnp.max(tiles[:, :, :128].astype(jnp.float32), axis=1).astype(jnp.int32)
    most = [jnp.zeros((1, 128), jnp.int32)] * 2
    for step in range(3):
        for side in range(2):
            n = step * 2 + side
            live = sections[n] >= 0
            most[side] = jnp.maximum(most[side], jnp.where(live, x[n : n + 1], 0))
    out[0:1] = most[0]
    out[1:2] = most[1]


def overflow(arrays, sections):
    out = pl.pallas_call(
        overflow_kernel,
        out_shape=jax.ShapeDtypeStruct((2, 128), jnp.int32),
        in_specs=[SMEM] + [ANY] * 6,
        out_specs=VMEM,
        scratch_shapes=[pltpu.VMEM((6, HEAD, B), jnp.bfloat16), pltpu.SemaphoreType.DMA((6,))],
        name="overflow",
    )(sections, *[arrays[n] for n in (0, 4, 8, 12, 16, 20)])
    return out[:, TOTAL] > SLOTS


ROUNDS = 3
C_BLOCKS = WINDOW * CAP
R_BLOCKS = WINDOW * PANEL * TC


def product_kernel(info, sections, *refs):
    arrays, refs = refs[: 24 * ROUNDS], refs[24 * ROUNDS :]
    accum, sums, left, right, at_row, at_k, counter, tiles, wide, heads, sems, head_sems = refs
    core = lax.rem(info[1], 2)
    counter[0] = 0
    counter[1] = 0

    def each_live(run):
        for r in range(ROUNDS):
            for step in range(3):
                for side in range(2):
                    is_c = core == side
                    section = sections[r * 6 + step + jnp.where(is_c, 0, 3)]

                    @pl.when(section >= 0)
                    def _():
                        for p in range(4):
                            run(r * 24 + step * 8 + side * 4 + p, is_c, section)

    def head_copy(n, is_c, section):
        return pltpu.make_async_copy(
            arrays[n].at[pl.ds(PS * B, HEAD)], tiles.at[n], head_sems.at[n]
        )

    each_live(lambda *at: head_copy(*at).start())

    @pl.loop(0, WINDOW * PANEL)
    def _(k):
        right[k] = jnp.zeros((B, TC * B), jnp.bfloat16)

    each_live(lambda *at: head_copy(*at).wait())
    wide[...] = jnp.max(tiles[:, :, :128].astype(jnp.float32), axis=1).astype(jnp.int32)
    copy = pltpu.make_async_copy(wide, heads, head_sems.at[0])
    copy.start()
    copy.wait()

    def fetch(n, is_c, section):
        @pl.loop(0, PS)
        def _(m):
            code = heads[n, m] - 1
            src = arrays[n].at[blocks_at(m)]

            @pl.when((code >= 0) & is_c)
            def _():
                c = counter[0]
                pltpu.make_async_copy(src, left.at[c], sems.at[c]).start()
                at_row[c] = code // TC
                at_k[c] = section * PANEL + lax.rem(code, TC)
                counter[0] = c + 1

            @pl.when((code >= 0) & jnp.logical_not(is_c) & (code // (PANEL * TC) == core))
            def _():
                c = counter[1]
                place = lax.rem(code, PANEL * TC)
                dst = right.at[section * PANEL + place // TC, :, blocks_at(lax.rem(place, TC))]
                pltpu.make_async_copy(src, dst, sems.at[C_BLOCKS + c]).start()
                counter[1] = c + 1

    each_live(fetch)

    @pl.loop(0, TR * B // 32)
    def _(s):
        accum[pl.ds(pl.multiple_of(s * 32, 32), 32), :] = jnp.zeros((32, TC * B), jnp.float32)

    def wait(n):
        pltpu.make_async_copy(arrays[0].at[pl.ds(0, B)], left.at[0], sems.at[n]).wait()

    @pl.loop(0, counter[1])
    def _(n):
        wait(C_BLOCKS + n)

    @pl.loop(0, counter[0])
    def _(n):
        wait(n)
        accum[blocks_at(at_row[n]), :] += jnp.dot(
            left[n], right[at_k[n]], preferred_element_type=jnp.float32
        )

    def add(s, total):
        x = accum[pl.ds(pl.multiple_of(s * 32, 32), 32), :]
        return total + jnp.sum((x * x).reshape(4, 8, TC * B), axis=0)

    total = lax.fori_loop(0, TR * B // 32, add, jnp.zeros((8, TC * B), jnp.float32))
    sums[...] = jnp.sum(total, axis=0, keepdims=True)


def products(info, sections, first, more):
    return pl.pallas_call(
        product_kernel,
        out_shape=(
            jax.ShapeDtypeStruct((TR * B, TC * B), jnp.float32),
            jax.ShapeDtypeStruct((1, TC * B), jnp.float32),
        ),
        in_specs=[SMEM] * 2 + [ANY] * len(first) + [HBM] * len(more),
        out_specs=(VMEM, VMEM),
        scratch_shapes=[
            pltpu.VMEM((C_BLOCKS, B, B), jnp.bfloat16),
            pltpu.VMEM((WINDOW * PANEL, B, TC * B), jnp.bfloat16),
            pltpu.SMEM((C_BLOCKS,), jnp.int32),
            pltpu.SMEM((C_BLOCKS,), jnp.int32),
            pltpu.SMEM((2,), jnp.int32),
            pltpu.VMEM((24 * ROUNDS, HEAD, B), jnp.bfloat16),
            pltpu.VMEM((24 * ROUNDS, 128), jnp.int32),
            pltpu.SMEM((24 * ROUNDS, 128), jnp.int32),
            pltpu.SemaphoreType.DMA((C_BLOCKS + R_BLOCKS,)),
            pltpu.SemaphoreType.DMA((24 * ROUNDS,)),
        ],
        compiler_params=pltpu.CompilerParams(vmem_limit_bytes=26 * 1024 * 1024),
        name="products",
    )(info, sections, *first, *more)


def scale_kernel(total, x, out, tiles, sems):
    factor = (TR * 8 * B) / (total[...] + EPS)

    def copy(r):
        slot = r % 2
        return pltpu.make_async_copy(tiles.at[slot], out.at[pl.ds(r * B, B)], sems.at[slot])

    for r in range(TR):
        if r >= 2:
            copy(r - 2).wait()

        @pl.loop(0, B // 16)
        def _(s, r=r):
            value = x[pl.ds(pl.multiple_of(r * B + s * 16, 16), 16), :]
            at = pl.ds(pl.multiple_of(s * 16, 16), 16)
            tiles[r % 2, at, :] = (value * value * factor).astype(jnp.bfloat16)

        copy(r).start()
    copy(TR - 2).wait()
    copy(TR - 1).wait()


def scale(total, expanded):
    return pl.pallas_call(
        scale_kernel,
        out_shape=jax.ShapeDtypeStruct((TR * B, TC * B), jnp.bfloat16),
        in_specs=[VMEM, VMEM],
        out_specs=ANY,
        scratch_shapes=[
            pltpu.VMEM((2, B, TC * B), jnp.bfloat16),
            pltpu.SemaphoreType.DMA((2,)),
        ],
        compiler_params=pltpu.CompilerParams(vmem_limit_bytes=16 * 1024 * 1024),
        name="scale",
    )(total, expanded)


def column_total(part):
    def turn(x, by):
        return lax.ppermute(x, "row", [(a, (a + 2 * by) % GRID_R) for a in range(GRID_R)])

    part = part + (turn(part, 1) + turn(part, 2) + turn(part, 3))
    return part + lax.ppermute(part, "row", [(a, a ^ 1) for a in range(GRID_R)])


def per_device(blocks, block_rows, block_cols, counts, sections):
    info = jnp.stack(
        [lax.axis_index("row"), lax.axis_index("col"), sections[0], sections[1], counts[0, 0]]
    ).astype(jnp.int32)
    args = (info, block_rows[0, 0], block_cols[0, 0], blocks[0, 0].reshape(CAP * B, B))
    first, to = send(0, "cr", *args)
    core = info[1] % 2
    mine = jnp.where(core == 0, to[:3], to[3:])
    theirs = jnp.where(core == 0, to[3:], to[:3])
    over = overflow(first, jnp.stack([mine, theirs], axis=1).reshape(6))
    c_over, r_over = over[core], over[1 - core]

    def again(*args, lanes):
        return send(SLOTS, lanes, *args)

    def nothing(*args):
        return unwritten(24, (ROWS, B)), jnp.full((6,), -1, jnp.int32)

    c_more, c_to = lax.cond(c_over, functools.partial(again, lanes="c"), nothing, *args)
    r_more, r_to = lax.cond(r_over, functools.partial(again, lanes="r"), nothing, *args)
    expanded, part = products(info, jnp.concatenate([to, c_to, r_to]), first, c_more + r_more)
    return scale(column_total(part), expanded)


def solution(mesh):
    in_specs = (
        P("row", "col", None, None, None),
        P("row", "col", None),
        P("row", "col", None),
        P("row", "col"),
        P(),
    )
    out_specs = P("row", "col")
    return jax.shard_map(
        per_device, mesh=mesh, in_specs=in_specs, out_specs=out_specs, check_vma=False
    )
```

```python
import functools

import jax
import jax.numpy as jnp
from jax import lax
from jax.experimental import pallas as pl
from jax.experimental.pallas import tpu as pltpu
from jax.sharding import PartitionSpec as P

B = 256
TC = 4
TR = 8
CAP = 32
WINDOW = 2
SECTIONS_ALL = 16
PANEL = 4
EPS = 1e-06

PIECE = 5
PIECE_MORE = 3
SLOTS = 4 * PIECE
HEAD = 16
TOTAL = 100

ANY = pl.BlockSpec(memory_space=pl.ANY)
VMEM = pl.BlockSpec(memory_space=pltpu.VMEM)
SMEM = pl.BlockSpec(memory_space=pltpu.SMEM)


def head_tile(values):
    lane = lax.broadcasted_iota(jnp.int32, (HEAD, B), 1)
    tile = jnp.zeros((HEAD, B), jnp.int32)
    for m, value in values:
        tile = jnp.where(lane == m, value, tile)
    return tile.astype(jnp.float32).astype(jnp.bfloat16)


def rows_of(ps):
    return ps * B + HEAD


def blocks_at(n):
    return pl.ds(pl.multiple_of(n * B, B), B)


def my_half(which, i, t0, t1):
    first = (i == t0 // 2) & (which == 0)
    return lax.rem(jnp.where(first, t0, t1), 2)


def c_code(rows, cols, slot):
    return rows[slot] * TC + cols[slot] + 1


def r_code(rows, cols, slot, core):
    return lax.rem(rows[slot], PANEL) * TC + cols[slot] + 1 + core * PANEL * TC


def pack_kernel(ps, offset, which, info, rows, cols, values, out, place, sems):
    i, j, t0, t1, count = info[0], info[1], info[2], info[3], info[4]
    core = lax.rem(j, 2)
    slots = 4 * ps

    def copy(slot, k):
        return pltpu.make_async_copy(
            values.at[blocks_at(slot)], out.at[blocks_at(k)], sems.at[k]
        )

    def finish(n, total):
        entries = [(k, place[k]) for k in range(slots)] + [(TOTAL, total)]
        out[slots * B :, :] = head_tile(entries)

        @pl.loop(0, n)
        def _(k):
            copy(0, k).wait()

    @pl.when((core == 1) & ((j == t0) | (j == t1)))
    def _():
        for k in range(slots):
            place[k] = 0
        n = jnp.clip(count - offset, 0, slots)

        @pl.loop(0, n)
        def _(k):
            place[k] = c_code(rows, cols, offset + k)
            copy(offset + k, k).start()

        finish(n, count)

    @pl.when((core == 0) & ((i == t0 // 2) | (i == t1 // 2)))
    def _():
        for k in range(slots):
            place[k] = 0
        half = my_half(which, i, t0, t1)

        def step(slot, seen):
            live = rows[slot] // PANEL == half

            @pl.when(live & (offset == 0))
            def _():
                place[seen] = r_code(rows, cols, slot, 0)
                copy(slot, seen).start()

            return seen + live.astype(jnp.int32)

        n = lax.fori_loop(0, count, step, jnp.int32(0))
        finish(n if offset == 0 else 0, n)


def pack(ps, offset, which, info, rows, cols, values):
    slots = 4 * ps
    return pl.pallas_call(
        functools.partial(pack_kernel, ps, offset, which),
        out_shape=jax.ShapeDtypeStruct((slots * B + HEAD, B), jnp.bfloat16),
        in_specs=[SMEM, SMEM, SMEM, ANY],
        out_specs=VMEM,
        scratch_shapes=[pltpu.SMEM((slots,), jnp.int32), pltpu.SemaphoreType.DMA((slots,))],
        compiler_params=pltpu.CompilerParams(vmem_limit_bytes=6 * 1024 * 1024),
        name="pack",
    )(info, rows, cols, values)


def arrange_kernel(ps, offset, which, info, rows, cols, values, got, *refs):
    outs, (place, tile, wide, heads, sems, head_sem) = refs[:4], refs[4:]
    i, j, t0, t1, count = info[0], info[1], info[2], info[3], info[4]
    core = lax.rem(j, 2)
    slots = 4 * ps
    position = jnp.where(core == 0, j // 4, i // 2)
    c_root = (core == 0) & ((j // 2 == t0 // 2) | (j // 2 == t1 // 2))
    r_root = (core == 1) & ((i == t0 // 2) | (i == t1 // 2))

    def start(src, q):
        away = lax.rem(q // ps - position + 4, 4)
        for by in range(4):

            @pl.when(away == by)
            def _():
                pltpu.make_async_copy(
                    src, outs[by].at[blocks_at(lax.rem(q, ps))], sems.at[q]
                ).start()

    def finish(n, total):
        head = head_tile([(q, place[q]) for q in range(slots)] + [(TOTAL, total)])
        for by in range(4):
            outs[by][ps * B :, :] = head

        @pl.loop(0, n)
        def _(q):
            pltpu.make_async_copy(
                values.at[pl.ds(0, B)], outs[0].at[pl.ds(0, B)], sems.at[q]
            ).wait()

    @pl.when(c_root | r_root)
    def _():
        for q in range(slots):
            place[q] = 0
        copy = pltpu.make_async_copy(got.at[pl.ds(slots * B, HEAD)], tile, head_sem)
        copy.start()
        copy.wait()
        wide[...] = tile[:8, :128].astype(jnp.float32).astype(jnp.int32)
        copy = pltpu.make_async_copy(wide, heads, head_sem)
        copy.start()
        copy.wait()

    @pl.when(c_root)
    def _():
        first = (j // 2 == t0 // 2) & (which == 0)
        own = lax.rem(jnp.where(first, t0, t1), 2) == 0
        total = jnp.where(own, count, heads[0, TOTAL])
        n = jnp.clip(total - offset, 0, slots)

        @pl.loop(0, n)
        def _(q):
            @pl.when(own)
            def _():
                place[q] = c_code(rows, cols, offset + q)
                start(values.at[blocks_at(offset + q)], q)

            @pl.when(jnp.logical_not(own))
            def _():
                place[q] = heads[0, q]
                start(got.at[blocks_at(q)], q)

        finish(n, total)

    @pl.when(r_root)
    def _():
        half = my_half(which, i, t0, t1)
        other = heads[0, TOTAL]

        @pl.loop(0, other if offset == 0 else 0)
        def _(k):
            q = k - offset

            @pl.when((q >= 0) & (q < slots))
            def _():
                place[q] = heads[0, k]
                start(got.at[blocks_at(k)], q)

        def step(slot, seen):
            live = rows[slot] // PANEL == half
            q = seen - offset

            @pl.when(live & (q >= 0) & (q < slots))
            def _():
                place[q] = r_code(rows, cols, slot, 1)
                start(values.at[blocks_at(slot)], q)

            return seen + live.astype(jnp.int32)

        total = lax.fori_loop(0, count, step, other)
        finish(jnp.clip(total - offset, 0, slots), total)


def arrange(ps, offset, which, info, rows, cols, values, got):
    slots = 4 * ps
    own, ahead, far, back = pl.pallas_call(
        functools.partial(arrange_kernel, ps, offset, which),
        out_shape=(jax.ShapeDtypeStruct((rows_of(ps), B), jnp.bfloat16),) * 4,
        in_specs=[SMEM, SMEM, SMEM, ANY, ANY],
        out_specs=(VMEM,) * 4,
        scratch_shapes=[
            pltpu.SMEM((slots,), jnp.int32),
            pltpu.VMEM((HEAD, B), jnp.bfloat16),
            pltpu.VMEM((8, 128), jnp.int32),
            pltpu.SMEM((8, 128), jnp.int32),
            pltpu.SemaphoreType.DMA((slots,)),
            pltpu.SemaphoreType.DMA,
        ],
        compiler_params=pltpu.CompilerParams(vmem_limit_bytes=54 * 1024 * 1024),
        name="arrange",
    )(info, rows, cols, values, got)
    return own, ahead, back, far


def unwritten(count, shape, dtype=jnp.bfloat16):
    return pl.pallas_call(
        lambda *refs: None,
        out_shape=(jax.ShapeDtypeStruct(shape, dtype),) * count,
        out_specs=(ANY,) * count,
        compiler_params=pltpu.CompilerParams(vmem_limit_bytes=1024 * 1024),
        name="unwritten",
    )()


GRID_R, GRID_C = 8, 16


def permute(x, to_c, to_r, lanes):
    pairs = []
    for i in range(GRID_R):
        for j in range(GRID_C):
            if j % 2 == 0 and "c" in lanes:
                pairs.append((i * GRID_C + j, i * GRID_C + to_c(j) % GRID_C))
            if j % 2 == 1 and "r" in lanes:
                pairs.append((i * GRID_C + j, to_r(i) % GRID_R * GRID_C + j))
    return lax.ppermute(x, ("row", "col"), pairs)


def shift(x, by, lanes):
    return permute(x, lambda j: j + 4 * by, lambda i: i + 2 * by, lanes)


def cross(x, lanes):
    return permute(x, lambda j: j ^ 2, lambda i: i ^ 1, lanes)


def swap_cores(x):
    return lax.ppermute(x, "col", [(a, a ^ 1) for a in range(GRID_C)])


def others(x, lanes):
    return [shift(x, 1, lanes), shift(x, -1, lanes), shift(x, 2, lanes)]


def send(ps, offset, lanes, info, rows, cols, values):
    i, j, t0, t1 = info[0], info[1], info[2], info[3]
    core = j % 2
    position = jnp.where(core == 0, j // 4, i // 2)
    one_root = t0 // 2 == t1 // 2
    plane0 = (t0 // 2) % 2
    same = plane0 == (t1 // 2) % 2
    at0 = jnp.where(core == 0, (j // 2) % 2, i % 2) == plane0

    def scatter(which):
        got = swap_cores(pack(ps, offset, which, info, rows, cols, values))
        own, ahead, back, far = arrange(ps, offset, which, info, rows, cols, values, got)
        ahead, back, far = shift(ahead, 1, lanes), shift(back, -1, lanes), shift(far, 2, lanes)

        def quarter(t):
            away = (position - t // 4 + 4) % 4
            return jnp.where(
                away == 0, own, jnp.where(away == 1, ahead, jnp.where(away == 2, far, back))
            )

        return quarter


    quarter = scatter(0)
    first = quarter(jnp.where(at0, t0, t1))
    extra = lax.cond(
        one_root, lambda: scatter(1)(t1), lambda: unwritten(1, first.shape)[0]
    )
    pieces, crossed = lax.optimization_barrier((others(first, lanes), cross(first, lanes)))
    pieces_a = [first] + pieces
    second = jnp.where(
        same & at0, jnp.where(one_root, extra, quarter(t1)), crossed
    )
    second_there = swap_cores(second)
    there_a = [swap_cores(p) for p in pieces_a]
    table, most = read_heads((0, 1), info, [first, there_a[0], second, second_there])
    pieces, crossed, there_a, table, most = lax.optimization_barrier(
        (others(second, lanes), cross(second, lanes), there_a, table, most)
    )
    step_a = pieces_a + there_a
    step_b = [second] + pieces + [second_there] + [swap_cores(p) for p in pieces]

    def more(x):
        pieces = [x] + others(x, lanes)
        there = [swap_cores(p) for p in pieces]
        return tuple(pieces + there), read_heads((2,), info, [x, there[0]])

    def no_more(x):
        return unwritten(8, x.shape), (
            unwritten(1, (2, 128), jnp.int32)[0],
            jnp.zeros((2,), jnp.int32),
        )

    step_c, (table_c, most_c) = lax.cond(same, more, no_more, crossed)
    arrays = tuple(step_a) + tuple(step_b) + tuple(step_c)
    return arrays, (table, table_c), jnp.maximum(most, most_c)


def section_of(info, step, is_c):
    i, j, t0, t1 = info[0], info[1], info[2], info[3]
    plane0, plane1 = lax.rem(t0 // 2, 2), lax.rem(t1 // 2, 2)
    same = plane0 == plane1
    at0 = jnp.where(is_c, lax.rem(j // 2, 2), lax.rem(i, 2)) == plane0
    if step == 0:
        return jnp.where(at0, 0, jnp.where(same, -1, 1))
    if step == 1:
        return jnp.where(at0, 1, 0)
    return jnp.where(same & jnp.logical_not(at0), 1, -1)


def heads_kernel(steps, info, *refs):
    count = 2 * len(steps)
    arrays, (table, out, tiles, sems) = refs[:count], refs[count:]
    copies = [
        pltpu.make_async_copy(a.at[pl.ds(a.shape[0] - HEAD, HEAD)], tiles.at[n], sems.at[n])
        for n, a in enumerate(arrays)
    ]
    for copy in copies:
        copy.start()
    for copy in copies:
        copy.wait()
    lane = lax.broadcasted_iota(jnp.int32, (count, 128), 1)
    x = jnp.max(tiles[:, :, :128].astype(jnp.float32), axis=1).astype(jnp.int32)
    table[...] = x
    x = jnp.where(lane == TOTAL, x, 0)
    core = lax.rem(info[1], 2)
    for kind in range(2):
        most = jnp.zeros((1, 128), jnp.int32)
        for n, step in enumerate(steps):
            live = section_of(info, step, kind == 0) >= 0
            row = jnp.where(core == kind, x[n * 2 : n * 2 + 1], x[n * 2 + 1 : n * 2 + 2])
            most = jnp.maximum(most, jnp.where(live, row, 0))
        out[kind] = jnp.max(most.astype(jnp.float32)).astype(jnp.int32)


def read_heads(steps, info, arrays):
    count = 2 * len(steps)
    return pl.pallas_call(
        functools.partial(heads_kernel, steps),
        out_shape=(
            jax.ShapeDtypeStruct((count, 128), jnp.int32),
            jax.ShapeDtypeStruct((2,), jnp.int32),
        ),
        in_specs=[SMEM] + [ANY] * count,
        out_specs=(VMEM, SMEM),
        scratch_shapes=[
            pltpu.VMEM((count, HEAD, B), jnp.bfloat16),
            pltpu.SemaphoreType.DMA((count,)),
        ],
        compiler_params=pltpu.CompilerParams(vmem_limit_bytes=2 * 1024 * 1024),
        name="heads",
    )(info, *arrays)


ROUNDS = 3
C_BLOCKS = WINDOW * CAP
R_BLOCKS = WINDOW * PANEL * TC


def product_kernel(info, most, *refs):
    tables, refs = refs[: 2 * ROUNDS], refs[2 * ROUNDS :]
    arrays, refs = refs[: 24 * ROUNDS], refs[24 * ROUNDS :]
    out, sums, accum, left, right, at_row, at_k, counter, sems, out_sems = refs
    i, j = info[0], info[1]
    core = lax.rem(j, 2)
    counter[0] = 0
    counter[1] = 0

    @pl.loop(0, WINDOW * PANEL)
    def _(k):
        right[k] = jnp.zeros((B, TC * B), jnp.bfloat16)

    def fetch(array, table, row, first, is_c, section):
        @pl.loop(0, array.shape[0] // B)
        def _(m):
            code = table[row, first + m] - 1
            src = array.at[blocks_at(m)]

            @pl.when((code >= 0) & is_c)
            def _():
                c = counter[0]
                pltpu.make_async_copy(src, left.at[c], sems.at[c]).start()
                at_row[c] = code // TC
                at_k[c] = section * PANEL + lax.rem(code, TC)
                counter[0] = c + 1

            @pl.when((code >= 0) & jnp.logical_not(is_c) & (code // (PANEL * TC) == core))
            def _():
                c = counter[1]
                place = lax.rem(code, PANEL * TC)
                dst = right.at[section * PANEL + place // TC, :, blocks_at(lax.rem(place, TC))]
                pltpu.make_async_copy(src, dst, sems.at[C_BLOCKS + c]).start()
                counter[1] = c + 1

    for r in range(ROUNDS):
        ps = PIECE if r == 0 else PIECE_MORE
        for step in range(3):
            for side in range(2):
                is_c = core == side
                section = section_of(info, step, is_c)
                live = section >= 0
                if r == 1:
                    live = live & is_c & (most[0] > SLOTS)
                if r == 2:
                    live = live & jnp.logical_not(is_c) & (most[1] > SLOTS)

                @pl.when(live)
                def _():
                    position = jnp.where(is_c, j // 4, i // 2)
                    table, row = tables[2 * r + step // 2], step % 2 * 2 + side
                    for p, by in enumerate((0, 3, 1, 2)):
                        first = lax.rem(position + by, 4) * ps
                        array = arrays[r * 24 + step * 8 + side * 4 + p]
                        fetch(array, table, row, first, is_c, section)

    @pl.loop(0, TR * B // 32)
    def _(s):
        accum[pl.ds(pl.multiple_of(s * 32, 32), 32), :] = jnp.zeros((32, TC * B), jnp.float32)

    def wait(n):
        pltpu.make_async_copy(arrays[0].at[pl.ds(0, B)], left.at[0], sems.at[n]).wait()

    @pl.loop(0, counter[1])
    def _(n):
        wait(C_BLOCKS + n)

    def multiply(n):
        accum[blocks_at(at_row[n]), :] += jnp.dot(
            left[n], right[at_k[n]], preferred_element_type=jnp.float32
        )

    count = counter[0]

    @pl.loop(0, count // 2)
    def _(n):
        wait(2 * n)
        wait(2 * n + 1)
        multiply(2 * n)
        multiply(2 * n + 1)

    @pl.when(lax.rem(count, 2) == 1)
    def _():
        wait(count - 1)
        multiply(count - 1)

    def out_copy(r):
        return pltpu.make_async_copy(
            accum.at[pl.ds(r * B, B)], out.at[pl.ds(r * B, B)], out_sems.at[r]
        )

    for r in range(TR):
        out_copy(r).start()

    def add(s, total):
        x = accum[pl.ds(pl.multiple_of(s * 32, 32), 32), :]
        return total + jnp.sum((x * x).reshape(4, 8, TC * B), axis=0)

    total = lax.fori_loop(0, TR * B // 32, add, jnp.zeros((8, TC * B), jnp.float32))
    sums[...] = jnp.sum(total, axis=0, keepdims=True)
    for r in range(TR):
        out_copy(r).wait()


def products(info, most, tables, first, more):
    return pl.pallas_call(
        product_kernel,
        out_shape=(
            jax.ShapeDtypeStruct((TR * B, TC * B), jnp.float32),
            jax.ShapeDtypeStruct((1, TC * B), jnp.float32),
        ),
        in_specs=[SMEM] * (2 + 2 * ROUNDS) + [ANY] * (len(first) + len(more)),
        out_specs=(ANY, VMEM),
        scratch_shapes=[
            pltpu.VMEM((TR * B, TC * B), jnp.float32),
            pltpu.VMEM((C_BLOCKS, B, B), jnp.bfloat16),
            pltpu.VMEM((WINDOW * PANEL, B, TC * B), jnp.bfloat16),
            pltpu.SMEM((C_BLOCKS,), jnp.int32),
            pltpu.SMEM((C_BLOCKS,), jnp.int32),
            pltpu.SMEM((2,), jnp.int32),
            pltpu.SemaphoreType.DMA((C_BLOCKS + R_BLOCKS,)),
            pltpu.SemaphoreType.DMA((TR,)),
        ],
        compiler_params=pltpu.CompilerParams(vmem_limit_bytes=58 * 1024 * 1024),
        name="products",
    )(info, most, *tables, *first, *more)


def scale_kernel(total, x, out, wide, tiles, in_sems, out_sems):
    def in_copy(r):
        return pltpu.make_async_copy(x.at[pl.ds(r * B, B)], wide.at[r], in_sems.at[r])

    def out_copy(r):
        return pltpu.make_async_copy(tiles.at[r], out.at[pl.ds(r * B, B)], out_sems.at[r])

    for r in range(TR):
        in_copy(r).start()
    factor = (TR * 8 * B) / (total[...] + EPS)
    for r in range(TR):
        in_copy(r).wait()

        @pl.loop(0, B // 32)
        def _(s, r=r):
            at = pl.ds(pl.multiple_of(s * 32, 32), 32)
            value = wide[r, at, :]
            tiles[r, at, :] = (value * value * factor).astype(jnp.bfloat16)

        out_copy(r).start()
    for r in range(TR):
        out_copy(r).wait()


def scale(total, expanded):
    return pl.pallas_call(
        scale_kernel,
        out_shape=jax.ShapeDtypeStruct((TR * B, TC * B), jnp.bfloat16),
        in_specs=[VMEM, ANY],
        out_specs=ANY,
        scratch_shapes=[
            pltpu.VMEM((TR, B, TC * B), jnp.float32),
            pltpu.VMEM((TR, B, TC * B), jnp.bfloat16),
            pltpu.SemaphoreType.DMA((TR,)),
            pltpu.SemaphoreType.DMA((TR,)),
        ],
        compiler_params=pltpu.CompilerParams(vmem_limit_bytes=58 * 1024 * 1024),
        name="scale",
    )(total, expanded)


def column_total(part):
    def turn(x, by):
        return lax.ppermute(x, "row", [(a, (a + 2 * by) % GRID_R) for a in range(GRID_R)])

    part = part + (turn(part, 1) + turn(part, 2) + turn(part, 3))
    return part + lax.ppermute(part, "row", [(a, a ^ 1) for a in range(GRID_R)])


def per_device(blocks, block_rows, block_cols, counts, sections):
    info = jnp.stack(
        [lax.axis_index("row"), lax.axis_index("col"), sections[0], sections[1], counts[0, 0]]
    ).astype(jnp.int32)
    args = (info, block_rows[0, 0], block_cols[0, 0], blocks[0, 0].reshape(CAP * B, B))
    first, tables, most = send(PIECE, 0, "cr", *args)

    def again(*args, lanes):
        return send(PIECE_MORE, SLOTS, lanes, *args)[:2]

    def nothing(*args):
        tables = unwritten(1, (4, 128), jnp.int32) + unwritten(1, (2, 128), jnp.int32)
        return unwritten(24, (rows_of(PIECE_MORE), B)), tables

    c_more, c_tables = lax.cond(most[0] > SLOTS, functools.partial(again, lanes="c"), nothing, *args)
    r_more, r_tables = lax.cond(most[1] > SLOTS, functools.partial(again, lanes="r"), nothing, *args)
    expanded, part = products(info, most, tables + c_tables + r_tables, first, c_more + r_more)
    return scale(column_total(part), expanded)


def solution(mesh):
    in_specs = (
        P("row", "col", None, None, None),
        P("row", "col", None),
        P("row", "col", None),
        P("row", "col"),
        P(),
    )
    out_specs = P("row", "col")
    return jax.shard_map(
        per_device, mesh=mesh, in_specs=in_specs, out_specs=out_specs, check_vma=False
    )
```

```python
import functools

import jax
import jax.numpy as jnp
from jax import lax
from jax.experimental import pallas as pl
from jax.experimental.pallas import tpu as pltpu
from jax.sharding import PartitionSpec as P

B = 256
TC = 4
TR = 8
CAP = 32
WINDOW = 2
SECTIONS_ALL = 16
PANEL = 4
EPS = 1e-06

PIECE = 8
HEAD = 16
TOTAL = 100

ANY = pl.BlockSpec(memory_space=pl.ANY)
VMEM = pl.BlockSpec(memory_space=pltpu.VMEM)
SMEM = pl.BlockSpec(memory_space=pltpu.SMEM)


def head_tile(values):
    lane = lax.broadcasted_iota(jnp.int32, (HEAD, B), 1)
    tile = jnp.zeros((HEAD, B), jnp.int32)
    for m, value in values:
        tile = jnp.where(lane == m, value, tile)
    return tile.astype(jnp.float32).astype(jnp.bfloat16)


def rows_of(ps):
    return ps * B + HEAD


def blocks_at(n):
    return pl.ds(pl.multiple_of(n * B, B), B)


def my_half(which, i, t0, t1):
    first = (i == t0 // 2) & (which == 0)
    return lax.rem(jnp.where(first, t0, t1), 2)


def c_code(rows, cols, slot):
    return rows[slot] * TC + cols[slot] + 1


def r_code(rows, cols, slot, core):
    return lax.rem(rows[slot], PANEL) * TC + cols[slot] + 1 + core * PANEL * TC


def pack_kernel(ps, offset, which, info, rows, cols, values, out, place, sems):
    i, j, t0, t1, count = info[0], info[1], info[2], info[3], info[4]
    core = lax.rem(j, 2)
    slots = 4 * ps

    def copy(slot, k):
        return pltpu.make_async_copy(
            values.at[blocks_at(slot)], out.at[blocks_at(k)], sems.at[k]
        )

    def finish(n, total):
        entries = [(k, place[k]) for k in range(slots)] + [(TOTAL, total)]
        out[slots * B :, :] = head_tile(entries)

        @pl.loop(0, n)
        def _(k):
            copy(0, k).wait()

    @pl.when((core == 1) & ((j == t0) | (j == t1)))
    def _():
        for k in range(slots):
            place[k] = 0
        n = jnp.clip(count - offset, 0, slots)

        @pl.loop(0, n)
        def _(k):
            place[k] = c_code(rows, cols, offset + k)
            copy(offset + k, k).start()

        finish(n, count)

    @pl.when((core == 0) & ((i == t0 // 2) | (i == t1 // 2)))
    def _():
        for k in range(slots):
            place[k] = 0
        half = my_half(which, i, t0, t1)

        def step(slot, seen):
            live = rows[slot] // PANEL == half

            @pl.when(live & (offset == 0))
            def _():
                place[seen] = r_code(rows, cols, slot, 0)
                copy(slot, seen).start()

            return seen + live.astype(jnp.int32)

        n = lax.fori_loop(0, count, step, jnp.int32(0))
        finish(n if offset == 0 else 0, n)


def pack(ps, offset, which, info, rows, cols, values):
    slots = 4 * ps
    return pl.pallas_call(
        functools.partial(pack_kernel, ps, offset, which),
        out_shape=jax.ShapeDtypeStruct((slots * B + HEAD, B), jnp.bfloat16),
        in_specs=[SMEM, SMEM, SMEM, ANY],
        out_specs=VMEM,
        scratch_shapes=[pltpu.SMEM((slots,), jnp.int32), pltpu.SemaphoreType.DMA((slots,))],
        compiler_params=pltpu.CompilerParams(vmem_limit_bytes=6 * 1024 * 1024),
        name="pack",
    )(info, rows, cols, values)


def arrange_kernel(ps, offset, which, info, rows, cols, values, got, *refs):
    outs, (place, tile, wide, heads, sems, head_sem) = refs[:4], refs[4:]
    i, j, t0, t1, count = info[0], info[1], info[2], info[3], info[4]
    core = lax.rem(j, 2)
    slots = 4 * ps
    position = jnp.where(core == 0, j // 4, i // 2)
    c_root = (core == 0) & ((j // 2 == t0 // 2) | (j // 2 == t1 // 2))
    r_root = (core == 1) & ((i == t0 // 2) | (i == t1 // 2))

    def start(src, q):
        away = lax.rem(q // ps - position + 4, 4)
        for by in range(4):

            @pl.when(away == by)
            def _():
                pltpu.make_async_copy(
                    src, outs[by].at[blocks_at(lax.rem(q, ps))], sems.at[q]
                ).start()

    def finish(n, total):
        head = head_tile([(q, place[q]) for q in range(slots)] + [(TOTAL, total)])
        for by in range(4):
            outs[by][ps * B :, :] = head

        @pl.loop(0, n)
        def _(q):
            pltpu.make_async_copy(
                values.at[pl.ds(0, B)], outs[0].at[pl.ds(0, B)], sems.at[q]
            ).wait()

    @pl.when(c_root | r_root)
    def _():
        for q in range(slots):
            place[q] = 0
        copy = pltpu.make_async_copy(got.at[pl.ds(slots * B, HEAD)], tile, head_sem)
        copy.start()
        copy.wait()
        wide[...] = tile[:8, :128].astype(jnp.float32).astype(jnp.int32)
        copy = pltpu.make_async_copy(wide, heads, head_sem)
        copy.start()
        copy.wait()

    @pl.when(c_root)
    def _():
        first = (j // 2 == t0 // 2) & (which == 0)
        own = lax.rem(jnp.where(first, t0, t1), 2) == 0
        total = jnp.where(own, count, heads[0, TOTAL])
        n = jnp.clip(total - offset, 0, slots)

        @pl.loop(0, n)
        def _(q):
            @pl.when(own)
            def _():
                place[q] = c_code(rows, cols, offset + q)
                start(values.at[blocks_at(offset + q)], q)

            @pl.when(jnp.logical_not(own))
            def _():
                place[q] = heads[0, q]
                start(got.at[blocks_at(q)], q)

        finish(n, total)

    @pl.when(r_root)
    def _():
        half = my_half(which, i, t0, t1)
        other = heads[0, TOTAL]

        @pl.loop(0, other if offset == 0 else 0)
        def _(k):
            q = k - offset

            @pl.when((q >= 0) & (q < slots))
            def _():
                place[q] = heads[0, k]
                start(got.at[blocks_at(k)], q)

        def step(slot, seen):
            live = rows[slot] // PANEL == half
            q = seen - offset

            @pl.when(live & (q >= 0) & (q < slots))
            def _():
                place[q] = r_code(rows, cols, slot, 1)
                start(values.at[blocks_at(slot)], q)

            return seen + live.astype(jnp.int32)

        total = lax.fori_loop(0, count, step, other)
        finish(jnp.clip(total - offset, 0, slots), total)


def arrange(ps, offset, which, info, rows, cols, values, got):
    slots = 4 * ps
    own, ahead, far, back = pl.pallas_call(
        functools.partial(arrange_kernel, ps, offset, which),
        out_shape=(jax.ShapeDtypeStruct((rows_of(ps), B), jnp.bfloat16),) * 4,
        in_specs=[SMEM, SMEM, SMEM, ANY, ANY],
        out_specs=(VMEM,) * 4,
        scratch_shapes=[
            pltpu.SMEM((slots,), jnp.int32),
            pltpu.VMEM((HEAD, B), jnp.bfloat16),
            pltpu.VMEM((8, 128), jnp.int32),
            pltpu.SMEM((8, 128), jnp.int32),
            pltpu.SemaphoreType.DMA((slots,)),
            pltpu.SemaphoreType.DMA,
        ],
        compiler_params=pltpu.CompilerParams(vmem_limit_bytes=54 * 1024 * 1024),
        name="arrange",
    )(info, rows, cols, values, got)
    return own, ahead, back, far


def unwritten(count, shape, dtype=jnp.bfloat16):
    return pl.pallas_call(
        lambda *refs: None,
        out_shape=(jax.ShapeDtypeStruct(shape, dtype),) * count,
        out_specs=(ANY,) * count,
        compiler_params=pltpu.CompilerParams(vmem_limit_bytes=1024 * 1024),
        name="unwritten",
    )()


GRID_R, GRID_C = 8, 16


def permute(x, to_c, to_r, lanes):
    pairs = []
    for i in range(GRID_R):
        for j in range(GRID_C):
            if j % 2 == 0 and "c" in lanes:
                pairs.append((i * GRID_C + j, i * GRID_C + to_c(j) % GRID_C))
            if j % 2 == 1 and "r" in lanes:
                pairs.append((i * GRID_C + j, to_r(i) % GRID_R * GRID_C + j))
    return lax.ppermute(x, ("row", "col"), pairs)


def shift(x, by, lanes):
    return permute(x, lambda j: j + 4 * by, lambda i: i + 2 * by, lanes)


def cross(x, lanes):
    return permute(x, lambda j: j ^ 2, lambda i: i ^ 1, lanes)


def swap_cores(x):
    return lax.ppermute(x, "col", [(a, a ^ 1) for a in range(GRID_C)])


def others(x, lanes):
    return [shift(x, 1, lanes), shift(x, -1, lanes), shift(x, 2, lanes)]


def send(ps, offset, lanes, info, rows, cols, values):
    i, j, t0, t1 = info[0], info[1], info[2], info[3]
    core = j % 2
    position = jnp.where(core == 0, j // 4, i // 2)
    one_root = t0 // 2 == t1 // 2
    plane0 = (t0 // 2) % 2
    same = plane0 == (t1 // 2) % 2
    at0 = jnp.where(core == 0, (j // 2) % 2, i % 2) == plane0

    def scatter(which):
        got = swap_cores(pack(ps, offset, which, info, rows, cols, values))
        own, ahead, back, far = arrange(ps, offset, which, info, rows, cols, values, got)
        ahead, back, far = shift(ahead, 1, lanes), shift(back, -1, lanes), shift(far, 2, lanes)

        def quarter(t):
            away = (position - t // 4 + 4) % 4
            return jnp.where(
                away == 0, own, jnp.where(away == 1, ahead, jnp.where(away == 2, far, back))
            )

        return quarter


    quarter = scatter(0)
    first = quarter(jnp.where(at0, t0, t1))
    extra = lax.cond(
        one_root, lambda: scatter(1)(t1), lambda: unwritten(1, first.shape)[0]
    )
    pieces, crossed = lax.optimization_barrier((others(first, lanes), cross(first, lanes)))
    pieces_a = [first] + pieces
    second = jnp.where(
        same & at0, jnp.where(one_root, extra, quarter(t1)), crossed
    )
    second_there = swap_cores(second)
    there_a = [swap_cores(p) for p in pieces_a]
    table, most = read_heads((0, 1), info, [first, there_a[0], second, second_there])
    pieces, crossed, there_a, table, most = lax.optimization_barrier(
        (others(second, lanes), cross(second, lanes), there_a, table, most)
    )
    step_a = pieces_a + there_a
    step_b = [second] + pieces + [second_there] + [swap_cores(p) for p in pieces]

    def more(x):
        pieces = [x] + others(x, lanes)
        there = [swap_cores(p) for p in pieces]
        return tuple(pieces + there), read_heads((2,), info, [x, there[0]])

    def no_more(x):
        return unwritten(8, x.shape), (
            unwritten(1, (2, 128), jnp.int32)[0],
            jnp.zeros((2,), jnp.int32),
        )

    step_c, (table_c, most_c) = lax.cond(same, more, no_more, crossed)
    arrays = tuple(step_a) + tuple(step_b) + tuple(step_c)
    return arrays, (table, table_c), jnp.maximum(most, most_c)


def section_of(info, step, is_c):
    i, j, t0, t1 = info[0], info[1], info[2], info[3]
    plane0, plane1 = lax.rem(t0 // 2, 2), lax.rem(t1 // 2, 2)
    same = plane0 == plane1
    at0 = jnp.where(is_c, lax.rem(j // 2, 2), lax.rem(i, 2)) == plane0
    if step == 0:
        return jnp.where(at0, 0, jnp.where(same, -1, 1))
    if step == 1:
        return jnp.where(at0, 1, 0)
    return jnp.where(same & jnp.logical_not(at0), 1, -1)


def heads_kernel(steps, info, *refs):
    count = 2 * len(steps)
    arrays, (table, out, tiles, sems) = refs[:count], refs[count:]
    copies = [
        pltpu.make_async_copy(a.at[pl.ds(a.shape[0] - HEAD, HEAD)], tiles.at[n], sems.at[n])
        for n, a in enumerate(arrays)
    ]
    for copy in copies:
        copy.start()
    for copy in copies:
        copy.wait()
    lane = lax.broadcasted_iota(jnp.int32, (count, 128), 1)
    x = jnp.max(tiles[:, :, :128].astype(jnp.float32), axis=1).astype(jnp.int32)
    table[...] = x
    x = jnp.where(lane == TOTAL, x, 0)
    core = lax.rem(info[1], 2)
    for kind in range(2):
        most = jnp.zeros((1, 128), jnp.int32)
        for n, step in enumerate(steps):
            live = section_of(info, step, kind == 0) >= 0
            row = jnp.where(core == kind, x[n * 2 : n * 2 + 1], x[n * 2 + 1 : n * 2 + 2])
            most = jnp.maximum(most, jnp.where(live, row, 0))
        out[kind] = jnp.max(most.astype(jnp.float32)).astype(jnp.int32)


def read_heads(steps, info, arrays):
    count = 2 * len(steps)
    return pl.pallas_call(
        functools.partial(heads_kernel, steps),
        out_shape=(
            jax.ShapeDtypeStruct((count, 128), jnp.int32),
            jax.ShapeDtypeStruct((2,), jnp.int32),
        ),
        in_specs=[SMEM] + [ANY] * count,
        out_specs=(VMEM, SMEM),
        scratch_shapes=[
            pltpu.VMEM((count, HEAD, B), jnp.bfloat16),
            pltpu.SemaphoreType.DMA((count,)),
        ],
        compiler_params=pltpu.CompilerParams(vmem_limit_bytes=2 * 1024 * 1024),
        name="heads",
    )(info, *arrays)


ROUNDS = 1
C_BLOCKS = WINDOW * CAP
R_BLOCKS = WINDOW * PANEL * TC


def product_kernel(info, *refs):
    tables, refs = refs[: 2 * ROUNDS], refs[2 * ROUNDS :]
    arrays, refs = refs[: 24 * ROUNDS], refs[24 * ROUNDS :]
    out, sums, accum, left, right, at_row, at_k, counter, sems, out_sems = refs
    i, j = info[0], info[1]
    core = lax.rem(j, 2)
    counter[0] = 0
    counter[1] = 0

    @pl.loop(0, WINDOW * PANEL)
    def _(k):
        right[k] = jnp.zeros((B, TC * B), jnp.bfloat16)

    def fetch(array, table, row, first, is_c, section):
        @pl.loop(0, array.shape[0] // B)
        def _(m):
            code = table[row, first + m] - 1
            src = array.at[blocks_at(m)]

            @pl.when((code >= 0) & is_c)
            def _():
                c = counter[0]
                pltpu.make_async_copy(src, left.at[c], sems.at[c]).start()
                at_row[c] = code // TC
                at_k[c] = section * PANEL + lax.rem(code, TC)
                counter[0] = c + 1

            @pl.when((code >= 0) & jnp.logical_not(is_c) & (code // (PANEL * TC) == core))
            def _():
                c = counter[1]
                place = lax.rem(code, PANEL * TC)
                dst = right.at[section * PANEL + place // TC, :, blocks_at(lax.rem(place, TC))]
                pltpu.make_async_copy(src, dst, sems.at[C_BLOCKS + c]).start()
                counter[1] = c + 1

    for r in range(ROUNDS):
        ps = PIECE
        for step in range(3):
            for side in range(2):
                is_c = core == side
                section = section_of(info, step, is_c)
                live = section >= 0

                @pl.when(live)
                def _():
                    position = jnp.where(is_c, j // 4, i // 2)
                    table, row = tables[2 * r + step // 2], step % 2 * 2 + side
                    for p, by in enumerate((0, 3, 1, 2)):
                        first = lax.rem(position + by, 4) * ps
                        array = arrays[r * 24 + step * 8 + side * 4 + p]
                        fetch(array, table, row, first, is_c, section)

    @pl.loop(0, TR * B // 32)
    def _(s):
        accum[pl.ds(pl.multiple_of(s * 32, 32), 32), :] = jnp.zeros((32, TC * B), jnp.float32)

    def wait(n):
        pltpu.make_async_copy(arrays[0].at[pl.ds(0, B)], left.at[0], sems.at[n]).wait()

    @pl.loop(0, counter[1])
    def _(n):
        wait(C_BLOCKS + n)

    def multiply(n):
        accum[blocks_at(at_row[n]), :] += jnp.dot(
            left[n], right[at_k[n]], preferred_element_type=jnp.float32
        )

    count = counter[0]

    @pl.loop(0, count // 2)
    def _(n):
        wait(2 * n)
        wait(2 * n + 1)
        multiply(2 * n)
        multiply(2 * n + 1)

    @pl.when(lax.rem(count, 2) == 1)
    def _():
        wait(count - 1)
        multiply(count - 1)

    def out_copy(r):
        return pltpu.make_async_copy(
            accum.at[pl.ds(r * B, B)], out.at[pl.ds(r * B, B)], out_sems.at[r]
        )

    for r in range(TR):
        out_copy(r).start()

    def add(s, total):
        x = accum[pl.ds(pl.multiple_of(s * 32, 32), 32), :]
        return total + jnp.sum((x * x).reshape(4, 8, TC * B), axis=0)

    total = lax.fori_loop(0, TR * B // 32, add, jnp.zeros((8, TC * B), jnp.float32))
    sums[...] = jnp.sum(total, axis=0, keepdims=True)
    for r in range(TR):
        out_copy(r).wait()


def products(info, tables, first):
    return pl.pallas_call(
        product_kernel,
        out_shape=(
            jax.ShapeDtypeStruct((TR * B, TC * B), jnp.float32),
            jax.ShapeDtypeStruct((1, TC * B), jnp.float32),
        ),
        in_specs=[SMEM] * (1 + 2 * ROUNDS) + [ANY] * len(first),
        out_specs=(ANY, VMEM),
        scratch_shapes=[
            pltpu.VMEM((TR * B, TC * B), jnp.float32),
            pltpu.VMEM((C_BLOCKS, B, B), jnp.bfloat16),
            pltpu.VMEM((WINDOW * PANEL, B, TC * B), jnp.bfloat16),
            pltpu.SMEM((C_BLOCKS,), jnp.int32),
            pltpu.SMEM((C_BLOCKS,), jnp.int32),
            pltpu.SMEM((2,), jnp.int32),
            pltpu.SemaphoreType.DMA((C_BLOCKS + R_BLOCKS,)),
            pltpu.SemaphoreType.DMA((TR,)),
        ],
        compiler_params=pltpu.CompilerParams(vmem_limit_bytes=58 * 1024 * 1024),
        name="products",
    )(info, *tables, *first)


def scale_kernel(total, x, out, wide, tiles, in_sems, out_sems):
    def in_copy(r):
        return pltpu.make_async_copy(x.at[pl.ds(r * B, B)], wide.at[r], in_sems.at[r])

    def out_copy(r):
        return pltpu.make_async_copy(tiles.at[r], out.at[pl.ds(r * B, B)], out_sems.at[r])

    for r in range(TR):
        in_copy(r).start()
    factor = (TR * 8 * B) / (total[...] + EPS)
    for r in range(TR):
        in_copy(r).wait()

        @pl.loop(0, B // 32)
        def _(s, r=r):
            at = pl.ds(pl.multiple_of(s * 32, 32), 32)
            value = wide[r, at, :]
            tiles[r, at, :] = (value * value * factor).astype(jnp.bfloat16)

        out_copy(r).start()
    for r in range(TR):
        out_copy(r).wait()


def scale(total, expanded):
    return pl.pallas_call(
        scale_kernel,
        out_shape=jax.ShapeDtypeStruct((TR * B, TC * B), jnp.bfloat16),
        in_specs=[VMEM, ANY],
        out_specs=ANY,
        scratch_shapes=[
            pltpu.VMEM((TR, B, TC * B), jnp.float32),
            pltpu.VMEM((TR, B, TC * B), jnp.bfloat16),
            pltpu.SemaphoreType.DMA((TR,)),
            pltpu.SemaphoreType.DMA((TR,)),
        ],
        compiler_params=pltpu.CompilerParams(vmem_limit_bytes=58 * 1024 * 1024),
        name="scale",
    )(total, expanded)


def column_total(part):
    def turn(x, by):
        return lax.ppermute(x, "row", [(a, (a + 2 * by) % GRID_R) for a in range(GRID_R)])

    part = part + (turn(part, 1) + turn(part, 2) + turn(part, 3))
    return part + lax.ppermute(part, "row", [(a, a ^ 1) for a in range(GRID_R)])


def per_device(blocks, block_rows, block_cols, counts, sections):
    info = jnp.stack(
        [lax.axis_index("row"), lax.axis_index("col"), sections[0], sections[1], counts[0, 0]]
    ).astype(jnp.int32)
    args = (info, block_rows[0, 0], block_cols[0, 0], blocks[0, 0].reshape(CAP * B, B))
    first, tables, _ = send(PIECE, 0, "cr", *args)

    expanded, part = products(info, tables, first)
    return scale(column_total(part), expanded)


def solution(mesh):
    in_specs = (
        P("row", "col", None, None, None),
        P("row", "col", None),
        P("row", "col", None),
        P("row", "col"),
        P(),
    )
    out_specs = P("row", "col")
    return jax.shard_map(
        per_device, mesh=mesh, in_specs=in_specs, out_specs=out_specs, check_vma=False
    )
```

```python
import functools

import jax
import jax.numpy as jnp
from jax import lax
from jax.experimental import pallas as pl
from jax.experimental.pallas import tpu as pltpu
from jax.sharding import PartitionSpec as P

B = 256
TC = 4
TR = 8
CAP = 32
WINDOW = 2
SECTIONS_ALL = 16
PANEL = 4
EPS = 1e-06

PIECE = 8
HEAD = 16
TOTAL = 100

ANY = pl.BlockSpec(memory_space=pl.ANY)
VMEM = pl.BlockSpec(memory_space=pltpu.VMEM)
SMEM = pl.BlockSpec(memory_space=pltpu.SMEM)


def head_tile(values):
    lane = lax.broadcasted_iota(jnp.int32, (HEAD, B), 1)
    tile = jnp.zeros((HEAD, B), jnp.int32)
    for m, value in values:
        tile = jnp.where(lane == m, value, tile)
    return tile.astype(jnp.float32).astype(jnp.bfloat16)


def rows_of(ps):
    return ps * B + HEAD


def blocks_at(n):
    return pl.ds(pl.multiple_of(n * B, B), B)


def my_half(which, i, t0, t1):
    first = (i == t0 // 2) & (which == 0)
    return lax.rem(jnp.where(first, t0, t1), 2)


def c_code(rows, cols, slot):
    return rows[slot] * TC + cols[slot] + 1


def r_code(rows, cols, slot, core):
    return lax.rem(rows[slot], PANEL) * TC + cols[slot] + 1 + core * PANEL * TC


def pack_kernel(ps, offset, which, info, rows, cols, values, out, place, sems):
    i, j, t0, t1, count = info[0], info[1], info[2], info[3], info[4]
    core = lax.rem(j, 2)
    slots = 4 * ps

    def copy(slot, k):
        return pltpu.make_async_copy(
            values.at[blocks_at(slot)], out.at[blocks_at(k)], sems.at[k]
        )

    def finish(n, total):
        entries = [(k, place[k]) for k in range(slots)] + [(TOTAL, total)]
        out[slots * B :, :] = head_tile(entries)

        @pl.loop(0, n)
        def _(k):
            copy(0, k).wait()

    @pl.when((core == 1) & ((j == t0) | (j == t1)))
    def _():
        for k in range(slots):
            place[k] = 0
        n = jnp.clip(count - offset, 0, slots)

        @pl.loop(0, n)
        def _(k):
            place[k] = c_code(rows, cols, offset + k)
            copy(offset + k, k).start()

        finish(n, count)

    @pl.when((core == 0) & ((i == t0 // 2) | (i == t1 // 2)))
    def _():
        for k in range(slots):
            place[k] = 0
        half = my_half(which, i, t0, t1)

        def step(slot, seen):
            live = rows[slot] // PANEL == half

            @pl.when(live & (offset == 0))
            def _():
                place[seen] = r_code(rows, cols, slot, 0)
                copy(slot, seen).start()

            return seen + live.astype(jnp.int32)

        n = lax.fori_loop(0, count, step, jnp.int32(0))
        finish(n if offset == 0 else 0, n)


def pack(ps, offset, which, info, rows, cols, values):
    slots = 4 * ps
    return pl.pallas_call(
        functools.partial(pack_kernel, ps, offset, which),
        out_shape=jax.ShapeDtypeStruct((slots * B + HEAD, B), jnp.bfloat16),
        in_specs=[SMEM, SMEM, SMEM, ANY],
        out_specs=VMEM,
        scratch_shapes=[pltpu.SMEM((slots,), jnp.int32), pltpu.SemaphoreType.DMA((slots,))],
        compiler_params=pltpu.CompilerParams(vmem_limit_bytes=6 * 1024 * 1024),
        name="pack",
    )(info, rows, cols, values)


def arrange_kernel(ps, offset, which, info, rows, cols, values, got, *refs):
    outs, (place, tile, wide, heads, sems, head_sem) = refs[:4], refs[4:]
    i, j, t0, t1, count = info[0], info[1], info[2], info[3], info[4]
    core = lax.rem(j, 2)
    slots = 4 * ps
    position = jnp.where(core == 0, j // 4, i // 2)
    c_root = (core == 0) & ((j // 2 == t0 // 2) | (j // 2 == t1 // 2))
    r_root = (core == 1) & ((i == t0 // 2) | (i == t1 // 2))

    def start(src, q):
        away = lax.rem(q // ps - position + 4, 4)
        for by in range(4):

            @pl.when(away == by)
            def _():
                pltpu.make_async_copy(
                    src, outs[by].at[blocks_at(lax.rem(q, ps))], sems.at[q]
                ).start()

    def finish(n, total):
        head = head_tile([(q, place[q]) for q in range(slots)] + [(TOTAL, total)])
        for by in range(4):
            outs[by][ps * B :, :] = head

        @pl.loop(0, n)
        def _(q):
            pltpu.make_async_copy(
                values.at[pl.ds(0, B)], outs[0].at[pl.ds(0, B)], sems.at[q]
            ).wait()

    @pl.when(c_root | r_root)
    def _():
        for q in range(slots):
            place[q] = 0
        copy = pltpu.make_async_copy(got.at[pl.ds(slots * B, HEAD)], tile, head_sem)
        copy.start()
        copy.wait()
        wide[...] = tile[:8, :128].astype(jnp.float32).astype(jnp.int32)
        copy = pltpu.make_async_copy(wide, heads, head_sem)
        copy.start()
        copy.wait()

    @pl.when(c_root)
    def _():
        first = (j // 2 == t0 // 2) & (which == 0)
        own = lax.rem(jnp.where(first, t0, t1), 2) == 0
        total = jnp.where(own, count, heads[0, TOTAL])
        n = jnp.clip(total - offset, 0, slots)

        @pl.loop(0, n)
        def _(q):
            @pl.when(own)
            def _():
                place[q] = c_code(rows, cols, offset + q)
                start(values.at[blocks_at(offset + q)], q)

            @pl.when(jnp.logical_not(own))
            def _():
                place[q] = heads[0, q]
                start(got.at[blocks_at(q)], q)

        finish(n, total)

    @pl.when(r_root)
    def _():
        half = my_half(which, i, t0, t1)
        other = heads[0, TOTAL]

        @pl.loop(0, other if offset == 0 else 0)
        def _(k):
            q = k - offset

            @pl.when((q >= 0) & (q < slots))
            def _():
                place[q] = heads[0, k]
                start(got.at[blocks_at(k)], q)

        def step(slot, seen):
            live = rows[slot] // PANEL == half
            q = seen - offset

            @pl.when(live & (q >= 0) & (q < slots))
            def _():
                place[q] = r_code(rows, cols, slot, 1)
                start(values.at[blocks_at(slot)], q)

            return seen + live.astype(jnp.int32)

        total = lax.fori_loop(0, count, step, other)
        finish(jnp.clip(total - offset, 0, slots), total)


def arrange(ps, offset, which, info, rows, cols, values, got):
    slots = 4 * ps
    own, ahead, far, back = pl.pallas_call(
        functools.partial(arrange_kernel, ps, offset, which),
        out_shape=(jax.ShapeDtypeStruct((rows_of(ps), B), jnp.bfloat16),) * 4,
        in_specs=[SMEM, SMEM, SMEM, ANY, ANY],
        out_specs=(VMEM,) * 4,
        scratch_shapes=[
            pltpu.SMEM((slots,), jnp.int32),
            pltpu.VMEM((HEAD, B), jnp.bfloat16),
            pltpu.VMEM((8, 128), jnp.int32),
            pltpu.SMEM((8, 128), jnp.int32),
            pltpu.SemaphoreType.DMA((slots,)),
            pltpu.SemaphoreType.DMA,
        ],
        compiler_params=pltpu.CompilerParams(vmem_limit_bytes=54 * 1024 * 1024),
        name="arrange",
    )(info, rows, cols, values, got)
    return own, ahead, back, far


def unwritten(count, shape, dtype=jnp.bfloat16):
    return pl.pallas_call(
        lambda *refs: None,
        out_shape=(jax.ShapeDtypeStruct(shape, dtype),) * count,
        out_specs=(ANY,) * count,
        compiler_params=pltpu.CompilerParams(vmem_limit_bytes=1024 * 1024),
        name="unwritten",
    )()


GRID_R, GRID_C = 8, 16


def permute(x, to_c, to_r, lanes):
    pairs = []
    for i in range(GRID_R):
        for j in range(GRID_C):
            if j % 2 == 0 and "c" in lanes:
                pairs.append((i * GRID_C + j, i * GRID_C + to_c(j) % GRID_C))
            if j % 2 == 1 and "r" in lanes:
                pairs.append((i * GRID_C + j, to_r(i) % GRID_R * GRID_C + j))
    return lax.ppermute(x, ("row", "col"), pairs)


def shift(x, by, lanes):
    return permute(x, lambda j: j + 4 * by, lambda i: i + 2 * by, lanes)


def cross(x, lanes):
    return permute(x, lambda j: j ^ 2, lambda i: i ^ 1, lanes)


def swap_cores(x):
    return lax.ppermute(x, "col", [(a, a ^ 1) for a in range(GRID_C)])


def others(x, lanes):
    return [shift(x, 1, lanes), shift(x, -1, lanes), shift(x, 2, lanes)]


def send(ps, offset, lanes, info, rows, cols, values):
    i, j, t0, t1 = info[0], info[1], info[2], info[3]
    core = j % 2
    position = jnp.where(core == 0, j // 4, i // 2)
    one_root = t0 // 2 == t1 // 2
    plane0 = (t0 // 2) % 2
    same = plane0 == (t1 // 2) % 2
    at0 = jnp.where(core == 0, (j // 2) % 2, i % 2) == plane0

    def scatter(which):
        got = swap_cores(pack(ps, offset, which, info, rows, cols, values))
        own, ahead, back, far = arrange(ps, offset, which, info, rows, cols, values, got)
        ahead, back, far = shift(ahead, 1, lanes), shift(back, -1, lanes), shift(far, 2, lanes)

        def quarter(t):
            away = (position - t // 4 + 4) % 4
            return jnp.where(
                away == 0, own, jnp.where(away == 1, ahead, jnp.where(away == 2, far, back))
            )

        return quarter


    quarter = scatter(0)
    first = quarter(jnp.where(at0, t0, t1))
    extra = lax.cond(
        one_root, lambda: scatter(1)(t1), lambda: unwritten(1, first.shape)[0]
    )
    pieces, crossed = lax.optimization_barrier((others(first, lanes), cross(first, lanes)))
    pieces_a = [first] + pieces
    second = jnp.where(
        same & at0, jnp.where(one_root, extra, quarter(t1)), crossed
    )
    second_there = swap_cores(second)
    there_a = [swap_cores(p) for p in pieces_a]
    table, most = read_heads((0, 1), info, [first, there_a[0], second, second_there])
    pieces = others(second, lanes)
    there = [swap_cores(p) for p in pieces[:2]]
    pieces, there, crossed, there_a, table, most = lax.optimization_barrier(
        (pieces, there, cross(second, lanes), there_a, table, most)
    )
    step_a = pieces_a + there_a
    step_b = [second] + pieces + [second_there] + there + [swap_cores(pieces[2])]

    def more(x):
        pieces = [x] + others(x, lanes)
        there = [swap_cores(p) for p in pieces]
        return tuple(pieces + there), read_heads((2,), info, [x, there[0]])

    def no_more(x):
        return unwritten(8, x.shape), (
            unwritten(1, (2, 128), jnp.int32)[0],
            jnp.zeros((2,), jnp.int32),
        )

    step_c, (table_c, most_c) = lax.cond(same, more, no_more, crossed)
    arrays = tuple(step_a) + tuple(step_b) + tuple(step_c)
    return arrays, (table, table_c), jnp.maximum(most, most_c)


def section_of(info, step, is_c):
    i, j, t0, t1 = info[0], info[1], info[2], info[3]
    plane0, plane1 = lax.rem(t0 // 2, 2), lax.rem(t1 // 2, 2)
    same = plane0 == plane1
    at0 = jnp.where(is_c, lax.rem(j // 2, 2), lax.rem(i, 2)) == plane0
    if step == 0:
        return jnp.where(at0, 0, jnp.where(same, -1, 1))
    if step == 1:
        return jnp.where(at0, 1, 0)
    return jnp.where(same & jnp.logical_not(at0), 1, -1)


def heads_kernel(steps, info, *refs):
    count = 2 * len(steps)
    arrays, (table, out, tiles, sems) = refs[:count], refs[count:]
    copies = [
        pltpu.make_async_copy(a.at[pl.ds(a.shape[0] - HEAD, HEAD)], tiles.at[n], sems.at[n])
        for n, a in enumerate(arrays)
    ]
    for copy in copies:
        copy.start()
    for copy in copies:
        copy.wait()
    lane = lax.broadcasted_iota(jnp.int32, (count, 128), 1)
    x = jnp.max(tiles[:, :, :128].astype(jnp.float32), axis=1).astype(jnp.int32)
    table[...] = x
    x = jnp.where(lane == TOTAL, x, 0)
    core = lax.rem(info[1], 2)
    for kind in range(2):
        most = jnp.zeros((1, 128), jnp.int32)
        for n, step in enumerate(steps):
            live = section_of(info, step, kind == 0) >= 0
            row = jnp.where(core == kind, x[n * 2 : n * 2 + 1], x[n * 2 + 1 : n * 2 + 2])
            most = jnp.maximum(most, jnp.where(live, row, 0))
        out[kind] = jnp.max(most.astype(jnp.float32)).astype(jnp.int32)


def read_heads(steps, info, arrays):
    count = 2 * len(steps)
    return pl.pallas_call(
        functools.partial(heads_kernel, steps),
        out_shape=(
            jax.ShapeDtypeStruct((count, 128), jnp.int32),
            jax.ShapeDtypeStruct((2,), jnp.int32),
        ),
        in_specs=[SMEM] + [ANY] * count,
        out_specs=(VMEM, SMEM),
        scratch_shapes=[
            pltpu.VMEM((count, HEAD, B), jnp.bfloat16),
            pltpu.SemaphoreType.DMA((count,)),
        ],
        compiler_params=pltpu.CompilerParams(vmem_limit_bytes=2 * 1024 * 1024),
        name="heads",
    )(info, *arrays)


ROUNDS = 1
C_BLOCKS = WINDOW * CAP
R_BLOCKS = WINDOW * PANEL * TC


def product_kernel(info, *refs):
    tables, refs = refs[: 2 * ROUNDS], refs[2 * ROUNDS :]
    arrays, refs = refs[: 24 * ROUNDS], refs[24 * ROUNDS :]
    out, sums, accum, left, right, at_row, at_k, counter, sems, out_sems = refs
    i, j = info[0], info[1]
    core = lax.rem(j, 2)
    counter[0] = 0
    counter[1] = 0

    @pl.loop(0, WINDOW * PANEL)
    def _(k):
        right[k] = jnp.zeros((B, TC * B), jnp.bfloat16)

    def fetch(array, table, row, first, is_c, section):
        @pl.loop(0, array.shape[0] // B)
        def _(m):
            code = table[row, first + m] - 1
            src = array.at[blocks_at(m)]

            @pl.when((code >= 0) & is_c)
            def _():
                c = counter[0]
                pltpu.make_async_copy(src, left.at[c], sems.at[c]).start()
                at_row[c] = code // TC
                at_k[c] = section * PANEL + lax.rem(code, TC)
                counter[0] = c + 1

            @pl.when((code >= 0) & jnp.logical_not(is_c) & (code // (PANEL * TC) == core))
            def _():
                c = counter[1]
                place = lax.rem(code, PANEL * TC)
                dst = right.at[section * PANEL + place // TC, :, blocks_at(lax.rem(place, TC))]
                pltpu.make_async_copy(src, dst, sems.at[C_BLOCKS + c]).start()
                counter[1] = c + 1

    for r in range(ROUNDS):
        ps = PIECE
        for step in range(3):
            for side in range(2):
                is_c = core == side
                section = section_of(info, step, is_c)
                live = section >= 0

                @pl.when(live)
                def _():
                    position = jnp.where(is_c, j // 4, i // 2)
                    table, row = tables[2 * r + step // 2], step % 2 * 2 + side
                    for p, by in enumerate((0, 3, 1, 2)):
                        first = lax.rem(position + by, 4) * ps
                        array = arrays[r * 24 + step * 8 + side * 4 + p]
                        fetch(array, table, row, first, is_c, section)

    @pl.loop(0, TR * B // 32)
    def _(s):
        accum[pl.ds(pl.multiple_of(s * 32, 32), 32), :] = jnp.zeros((32, TC * B), jnp.float32)

    def wait(n):
        pltpu.make_async_copy(arrays[0].at[pl.ds(0, B)], left.at[0], sems.at[n]).wait()

    @pl.loop(0, counter[1])
    def _(n):
        wait(C_BLOCKS + n)

    def multiply(n):
        accum[blocks_at(at_row[n]), :] += jnp.dot(
            left[n], right[at_k[n]], preferred_element_type=jnp.float32
        )

    count = counter[0]

    @pl.loop(0, count // 4)
    def _(n):
        for m in range(4):
            wait(4 * n + m)
        for m in range(4):
            multiply(4 * n + m)

    @pl.loop(count // 4 * 4, count)
    def _(n):
        wait(n)
        multiply(n)

    def out_copy(r):
        return pltpu.make_async_copy(
            accum.at[pl.ds(r * B, B)], out.at[pl.ds(r * B, B)], out_sems.at[r]
        )

    for r in range(TR):
        out_copy(r).start()

    def add(s, total):
        x = accum[pl.ds(pl.multiple_of(s * 32, 32), 32), :]
        return total + jnp.sum((x * x).reshape(4, 8, TC * B), axis=0)

    total = lax.fori_loop(0, TR * B // 32, add, jnp.zeros((8, TC * B), jnp.float32))
    sums[...] = jnp.sum(total, axis=0, keepdims=True)
    for r in range(TR):
        out_copy(r).wait()


def products(info, tables, first):
    return pl.pallas_call(
        product_kernel,
        out_shape=(
            jax.ShapeDtypeStruct((TR * B, TC * B), jnp.float32),
            jax.ShapeDtypeStruct((1, TC * B), jnp.float32),
        ),
        in_specs=[SMEM] * (1 + 2 * ROUNDS) + [ANY] * len(first),
        out_specs=(ANY, VMEM),
        scratch_shapes=[
            pltpu.VMEM((TR * B, TC * B), jnp.float32),
            pltpu.VMEM((C_BLOCKS, B, B), jnp.bfloat16),
            pltpu.VMEM((WINDOW * PANEL, B, TC * B), jnp.bfloat16),
            pltpu.SMEM((C_BLOCKS,), jnp.int32),
            pltpu.SMEM((C_BLOCKS,), jnp.int32),
            pltpu.SMEM((2,), jnp.int32),
            pltpu.SemaphoreType.DMA((C_BLOCKS + R_BLOCKS,)),
            pltpu.SemaphoreType.DMA((TR,)),
        ],
        compiler_params=pltpu.CompilerParams(vmem_limit_bytes=58 * 1024 * 1024),
        name="products",
    )(info, *tables, *first)


def scale_kernel(total, x, out, wide, tiles, in_sems, out_sems):
    def in_copy(r):
        return pltpu.make_async_copy(x.at[pl.ds(r * B, B)], wide.at[r], in_sems.at[r])

    def out_copy(r):
        return pltpu.make_async_copy(tiles.at[r], out.at[pl.ds(r * B, B)], out_sems.at[r])

    for r in range(TR):
        in_copy(r).start()
    factor = (TR * 8 * B) / (total[...] + EPS)
    for r in range(TR):
        in_copy(r).wait()

        @pl.loop(0, B // 32)
        def _(s, r=r):
            at = pl.ds(pl.multiple_of(s * 32, 32), 32)
            value = wide[r, at, :]
            tiles[r, at, :] = (value * value * factor).astype(jnp.bfloat16)

        out_copy(r).start()
    for r in range(TR):
        out_copy(r).wait()


def scale(total, expanded):
    return pl.pallas_call(
        scale_kernel,
        out_shape=jax.ShapeDtypeStruct((TR * B, TC * B), jnp.bfloat16),
        in_specs=[VMEM, ANY],
        out_specs=ANY,
        scratch_shapes=[
            pltpu.VMEM((TR, B, TC * B), jnp.float32),
            pltpu.VMEM((TR, B, TC * B), jnp.bfloat16),
            pltpu.SemaphoreType.DMA((TR,)),
            pltpu.SemaphoreType.DMA((TR,)),
        ],
        compiler_params=pltpu.CompilerParams(vmem_limit_bytes=58 * 1024 * 1024),
        name="scale",
    )(total, expanded)


def column_total(part):
    def turn(x, by):
        return lax.ppermute(x, "row", [(a, (a + 2 * by) % GRID_R) for a in range(GRID_R)])

    part = part + (turn(part, 1) + turn(part, 2) + turn(part, 3))
    return part + lax.ppermute(part, "row", [(a, a ^ 1) for a in range(GRID_R)])


def per_device(blocks, block_rows, block_cols, counts, sections):
    info = jnp.stack(
        [lax.axis_index("row"), lax.axis_index("col"), sections[0], sections[1], counts[0, 0]]
    ).astype(jnp.int32)
    args = (info, block_rows[0, 0], block_cols[0, 0], blocks[0, 0].reshape(CAP * B, B))
    first, tables, _ = send(PIECE, 0, "cr", *args)

    expanded, part = products(info, tables, first)
    return scale(column_total(part), expanded)


def solution(mesh):
    in_specs = (
        P("row", "col", None, None, None),
        P("row", "col", None),
        P("row", "col", None),
        P("row", "col"),
        P(),
    )
    out_specs = P("row", "col")
    return jax.shard_map(
        per_device, mesh=mesh, in_specs=in_specs, out_specs=out_specs, check_vma=False
    )
```

```python
import functools

import jax
import jax.numpy as jnp
from jax import lax
from jax.experimental import pallas as pl
from jax.experimental.pallas import tpu as pltpu
from jax.sharding import PartitionSpec as P

B = 256
TC = 4
TR = 8
CAP = 32
WINDOW = 2
SECTIONS_ALL = 16
PANEL = 4
EPS = 1e-06

PIECE = 8
HEAD = 16
TOTAL = 100

ANY = pl.BlockSpec(memory_space=pl.ANY)
VMEM = pl.BlockSpec(memory_space=pltpu.VMEM)
SMEM = pl.BlockSpec(memory_space=pltpu.SMEM)


def head_tile(values):
    lane = lax.broadcasted_iota(jnp.int32, (HEAD, B), 1)
    tile = jnp.zeros((HEAD, B), jnp.int32)
    for m, value in values:
        tile = jnp.where(lane == m, value, tile)
    return tile.astype(jnp.float32).astype(jnp.bfloat16)


def rows_of(ps):
    return ps * B + HEAD


def blocks_at(n):
    return pl.ds(pl.multiple_of(n * B, B), B)


def my_half(which, i, t0, t1):
    first = (i == t0 // 2) & (which == 0)
    return lax.rem(jnp.where(first, t0, t1), 2)


def c_code(rows, cols, slot):
    return rows[slot] * TC + cols[slot] + 1


def r_code(rows, cols, slot, core):
    return lax.rem(rows[slot], PANEL) * TC + cols[slot] + 1 + core * PANEL * TC


def pack_kernel(ps, offset, which, info, rows, cols, values, out, place, sems):
    i, j, t0, t1, count = info[0], info[1], info[2], info[3], info[4]
    core = lax.rem(j, 2)
    slots = 4 * ps

    def copy(slot, k):
        return pltpu.make_async_copy(
            values.at[blocks_at(slot)], out.at[blocks_at(k)], sems.at[k]
        )

    def finish(n, total):
        entries = [(k, place[k]) for k in range(slots)] + [(TOTAL, total)]
        out[slots * B :, :] = head_tile(entries)

        @pl.loop(0, n)
        def _(k):
            copy(0, k).wait()

    @pl.when((core == 1) & ((j == t0) | (j == t1)))
    def _():
        for k in range(slots):
            place[k] = 0
        n = jnp.clip(count - offset, 0, slots)

        @pl.loop(0, n)
        def _(k):
            place[k] = c_code(rows, cols, offset + k)
            copy(offset + k, k).start()

        finish(n, count)

    @pl.when((core == 0) & ((i == t0 // 2) | (i == t1 // 2)))
    def _():
        for k in range(slots):
            place[k] = 0
        half = my_half(which, i, t0, t1)

        def step(slot, seen):
            live = rows[slot] // PANEL == half

            @pl.when(live & (offset == 0))
            def _():
                place[seen] = r_code(rows, cols, slot, 0)
                copy(slot, seen).start()

            return seen + live.astype(jnp.int32)

        n = lax.fori_loop(0, count, step, jnp.int32(0))
        finish(n if offset == 0 else 0, n)


def pack(ps, offset, which, info, rows, cols, values):
    slots = 4 * ps
    return pl.pallas_call(
        functools.partial(pack_kernel, ps, offset, which),
        out_shape=jax.ShapeDtypeStruct((slots * B + HEAD, B), jnp.bfloat16),
        in_specs=[SMEM, SMEM, SMEM, ANY],
        out_specs=VMEM,
        scratch_shapes=[pltpu.SMEM((slots,), jnp.int32), pltpu.SemaphoreType.DMA((slots,))],
        compiler_params=pltpu.CompilerParams(vmem_limit_bytes=6 * 1024 * 1024),
        name="pack",
    )(info, rows, cols, values)


def arrange_kernel(ps, offset, which, info, rows, cols, values, got, *refs):
    outs, (place, tile, wide, heads, sems, head_sem) = refs[:4], refs[4:]
    i, j, t0, t1, count = info[0], info[1], info[2], info[3], info[4]
    core = lax.rem(j, 2)
    slots = 4 * ps
    position = jnp.where(core == 0, j // 4, i // 2)
    c_root = (core == 0) & ((j // 2 == t0 // 2) | (j // 2 == t1 // 2))
    r_root = (core == 1) & ((i == t0 // 2) | (i == t1 // 2))

    def start(src, q):
        away = lax.rem(q // ps - position + 4, 4)
        for by in range(4):

            @pl.when(away == by)
            def _():
                pltpu.make_async_copy(
                    src, outs[by].at[blocks_at(lax.rem(q, ps))], sems.at[q]
                ).start()

    def finish(n, total):
        head = head_tile([(q, place[q]) for q in range(slots)] + [(TOTAL, total)])
        for by in range(4):
            outs[by][ps * B :, :] = head

        @pl.loop(0, n)
        def _(q):
            pltpu.make_async_copy(
                values.at[pl.ds(0, B)], outs[0].at[pl.ds(0, B)], sems.at[q]
            ).wait()

    @pl.when(c_root | r_root)
    def _():
        for q in range(slots):
            place[q] = 0
        copy = pltpu.make_async_copy(got.at[pl.ds(slots * B, HEAD)], tile, head_sem)
        copy.start()
        copy.wait()
        wide[...] = tile[:8, :128].astype(jnp.float32).astype(jnp.int32)
        copy = pltpu.make_async_copy(wide, heads, head_sem)
        copy.start()
        copy.wait()

    @pl.when(c_root)
    def _():
        first = (j // 2 == t0 // 2) & (which == 0)
        own = lax.rem(jnp.where(first, t0, t1), 2) == 0
        total = jnp.where(own, count, heads[0, TOTAL])
        n = jnp.clip(total - offset, 0, slots)

        @pl.loop(0, n)
        def _(q):
            @pl.when(own)
            def _():
                place[q] = c_code(rows, cols, offset + q)
                start(values.at[blocks_at(offset + q)], q)

            @pl.when(jnp.logical_not(own))
            def _():
                place[q] = heads[0, q]
                start(got.at[blocks_at(q)], q)

        finish(n, total)

    @pl.when(r_root)
    def _():
        half = my_half(which, i, t0, t1)
        other = heads[0, TOTAL]

        @pl.loop(0, other if offset == 0 else 0)
        def _(k):
            q = k - offset

            @pl.when((q >= 0) & (q < slots))
            def _():
                place[q] = heads[0, k]
                start(got.at[blocks_at(k)], q)

        def step(slot, seen):
            live = rows[slot] // PANEL == half
            q = seen - offset

            @pl.when(live & (q >= 0) & (q < slots))
            def _():
                place[q] = r_code(rows, cols, slot, 1)
                start(values.at[blocks_at(slot)], q)

            return seen + live.astype(jnp.int32)

        total = lax.fori_loop(0, count, step, other)
        finish(jnp.clip(total - offset, 0, slots), total)


def arrange(ps, offset, which, info, rows, cols, values, got):
    slots = 4 * ps
    own, ahead, far, back = pl.pallas_call(
        functools.partial(arrange_kernel, ps, offset, which),
        out_shape=(jax.ShapeDtypeStruct((rows_of(ps), B), jnp.bfloat16),) * 4,
        in_specs=[SMEM, SMEM, SMEM, ANY, ANY],
        out_specs=(VMEM,) * 4,
        scratch_shapes=[
            pltpu.SMEM((slots,), jnp.int32),
            pltpu.VMEM((HEAD, B), jnp.bfloat16),
            pltpu.VMEM((8, 128), jnp.int32),
            pltpu.SMEM((8, 128), jnp.int32),
            pltpu.SemaphoreType.DMA((slots,)),
            pltpu.SemaphoreType.DMA,
        ],
        compiler_params=pltpu.CompilerParams(vmem_limit_bytes=54 * 1024 * 1024),
        name="arrange",
    )(info, rows, cols, values, got)
    return own, ahead, back, far


def unwritten(count, shape, dtype=jnp.bfloat16):
    return pl.pallas_call(
        lambda *refs: None,
        out_shape=(jax.ShapeDtypeStruct(shape, dtype),) * count,
        out_specs=(ANY,) * count,
        compiler_params=pltpu.CompilerParams(vmem_limit_bytes=1024 * 1024),
        name="unwritten",
    )()


GRID_R, GRID_C = 8, 16


def permute(x, to_c, to_r, lanes):
    pairs = []
    for i in range(GRID_R):
        for j in range(GRID_C):
            if j % 2 == 0 and "c" in lanes:
                pairs.append((i * GRID_C + j, i * GRID_C + to_c(j) % GRID_C))
            if j % 2 == 1 and "r" in lanes:
                pairs.append((i * GRID_C + j, to_r(i) % GRID_R * GRID_C + j))
    return lax.ppermute(x, ("row", "col"), pairs)


def shift(x, by, lanes):
    return permute(x, lambda j: j + 4 * by, lambda i: i + 2 * by, lanes)


def cross(x, lanes):
    return permute(x, lambda j: j ^ 2, lambda i: i ^ 1, lanes)


def swap_cores(x):
    return lax.ppermute(x, "col", [(a, a ^ 1) for a in range(GRID_C)])


def others(x, lanes):
    return [shift(x, 1, lanes), shift(x, -1, lanes), shift(x, 2, lanes)]


def send(ps, offset, lanes, info, rows, cols, values):
    i, j, t0, t1 = info[0], info[1], info[2], info[3]
    core = j % 2
    position = jnp.where(core == 0, j // 4, i // 2)
    one_root = t0 // 2 == t1 // 2
    plane0 = (t0 // 2) % 2
    same = plane0 == (t1 // 2) % 2
    at0 = jnp.where(core == 0, (j // 2) % 2, i % 2) == plane0

    def scatter(which):
        got = swap_cores(pack(ps, offset, which, info, rows, cols, values))
        own, ahead, back, far = arrange(ps, offset, which, info, rows, cols, values, got)
        ahead, back, far = shift(ahead, 1, lanes), shift(back, -1, lanes), shift(far, 2, lanes)

        def quarter(t):
            away = (position - t // 4 + 4) % 4
            return jnp.where(
                away == 0, own, jnp.where(away == 1, ahead, jnp.where(away == 2, far, back))
            )

        return quarter


    quarter = scatter(0)
    first = quarter(jnp.where(at0, t0, t1))
    extra = lax.cond(
        one_root, lambda: scatter(1)(t1), lambda: unwritten(1, first.shape)[0]
    )
    pieces, crossed, first_there = lax.optimization_barrier(
        (others(first, lanes), cross(first, lanes), swap_cores(first))
    )
    pieces_a = [first] + pieces
    second = jnp.where(
        same & at0, jnp.where(one_root, extra, quarter(t1)), crossed
    )
    second_there = swap_cores(second)
    there_a = [first_there] + [swap_cores(p) for p in pieces_a[1:]]
    table, most = read_heads((0, 1), info, [first, there_a[0], second, second_there])
    pieces = others(second, lanes)
    there = [swap_cores(p) for p in pieces[:2]]
    pieces, there, crossed, there_a, table, most = lax.optimization_barrier(
        (pieces, there, cross(second, lanes), there_a, table, most)
    )
    step_a = pieces_a + there_a
    step_b = [second] + pieces + [second_there] + there + [swap_cores(pieces[2])]

    def more(x):
        pieces = [x] + others(x, lanes)
        there = [swap_cores(p) for p in pieces]
        return tuple(pieces + there), read_heads((2,), info, [x, there[0]])

    def no_more(x):
        return unwritten(8, x.shape), (
            unwritten(1, (2, 128), jnp.int32)[0],
            jnp.zeros((2,), jnp.int32),
        )

    step_c, (table_c, most_c) = lax.cond(same, more, no_more, crossed)
    arrays = tuple(step_a) + tuple(step_b) + tuple(step_c)
    return arrays, (table, table_c), jnp.maximum(most, most_c)


def section_of(info, step, is_c):
    i, j, t0, t1 = info[0], info[1], info[2], info[3]
    plane0, plane1 = lax.rem(t0 // 2, 2), lax.rem(t1 // 2, 2)
    same = plane0 == plane1
    at0 = jnp.where(is_c, lax.rem(j // 2, 2), lax.rem(i, 2)) == plane0
    if step == 0:
        return jnp.where(at0, 0, jnp.where(same, -1, 1))
    if step == 1:
        return jnp.where(at0, 1, 0)
    return jnp.where(same & jnp.logical_not(at0), 1, -1)


def heads_kernel(steps, info, *refs):
    count = 2 * len(steps)
    arrays, (table, out, tiles, sems) = refs[:count], refs[count:]
    copies = [
        pltpu.make_async_copy(a.at[pl.ds(a.shape[0] - HEAD, HEAD)], tiles.at[n], sems.at[n])
        for n, a in enumerate(arrays)
    ]
    for copy in copies:
        copy.start()
    for copy in copies:
        copy.wait()
    lane = lax.broadcasted_iota(jnp.int32, (count, 128), 1)
    x = jnp.max(tiles[:, :, :128].astype(jnp.float32), axis=1).astype(jnp.int32)
    table[...] = x
    x = jnp.where(lane == TOTAL, x, 0)
    core = lax.rem(info[1], 2)
    for kind in range(2):
        most = jnp.zeros((1, 128), jnp.int32)
        for n, step in enumerate(steps):
            live = section_of(info, step, kind == 0) >= 0
            row = jnp.where(core == kind, x[n * 2 : n * 2 + 1], x[n * 2 + 1 : n * 2 + 2])
            most = jnp.maximum(most, jnp.where(live, row, 0))
        out[kind] = jnp.max(most.astype(jnp.float32)).astype(jnp.int32)


def read_heads(steps, info, arrays):
    count = 2 * len(steps)
    return pl.pallas_call(
        functools.partial(heads_kernel, steps),
        out_shape=(
            jax.ShapeDtypeStruct((count, 128), jnp.int32),
            jax.ShapeDtypeStruct((2,), jnp.int32),
        ),
        in_specs=[SMEM] + [ANY] * count,
        out_specs=(VMEM, SMEM),
        scratch_shapes=[
            pltpu.VMEM((count, HEAD, B), jnp.bfloat16),
            pltpu.SemaphoreType.DMA((count,)),
        ],
        compiler_params=pltpu.CompilerParams(vmem_limit_bytes=2 * 1024 * 1024),
        name="heads",
    )(info, *arrays)


ROUNDS = 1
C_BLOCKS = WINDOW * CAP
R_BLOCKS = WINDOW * PANEL * TC


def product_kernel(info, *refs):
    tables, refs = refs[: 2 * ROUNDS], refs[2 * ROUNDS :]
    arrays, refs = refs[: 24 * ROUNDS], refs[24 * ROUNDS :]
    out, sums, accum, left, right, at_row, at_k, counter, sems, out_sems = refs
    i, j = info[0], info[1]
    core = lax.rem(j, 2)
    counter[0] = 0
    counter[1] = 0

    @pl.loop(0, WINDOW * PANEL)
    def _(k):
        right[k] = jnp.zeros((B, TC * B), jnp.bfloat16)

    def fetch(array, table, row, first, is_c, section):
        @pl.loop(0, array.shape[0] // B)
        def _(m):
            code = table[row, first + m] - 1
            src = array.at[blocks_at(m)]

            @pl.when((code >= 0) & is_c)
            def _():
                c = counter[0]
                pltpu.make_async_copy(src, left.at[c], sems.at[c]).start()
                at_row[c] = code // TC
                at_k[c] = section * PANEL + lax.rem(code, TC)
                counter[0] = c + 1

            @pl.when((code >= 0) & jnp.logical_not(is_c) & (code // (PANEL * TC) == core))
            def _():
                c = counter[1]
                place = lax.rem(code, PANEL * TC)
                dst = right.at[section * PANEL + place // TC, :, blocks_at(lax.rem(place, TC))]
                pltpu.make_async_copy(src, dst, sems.at[C_BLOCKS + c]).start()
                counter[1] = c + 1

    for r in range(ROUNDS):
        ps = PIECE
        for step in range(3):
            for side in range(2):
                is_c = core == side
                section = section_of(info, step, is_c)
                live = section >= 0

                @pl.when(live)
                def _():
                    position = jnp.where(is_c, j // 4, i // 2)
                    table, row = tables[2 * r + step // 2], step % 2 * 2 + side
                    for p, by in enumerate((0, 3, 1, 2)):
                        first = lax.rem(position + by, 4) * ps
                        array = arrays[r * 24 + step * 8 + side * 4 + p]
                        fetch(array, table, row, first, is_c, section)

    @pl.loop(0, TR * B // 32)
    def _(s):
        accum[pl.ds(pl.multiple_of(s * 32, 32), 32), :] = jnp.zeros((32, TC * B), jnp.float32)

    def wait(n):
        pltpu.make_async_copy(arrays[0].at[pl.ds(0, B)], left.at[0], sems.at[n]).wait()

    @pl.loop(0, counter[1])
    def _(n):
        wait(C_BLOCKS + n)

    def multiply(n):
        accum[blocks_at(at_row[n]), :] += jnp.dot(
            left[n], right[at_k[n]], preferred_element_type=jnp.float32
        )

    count = counter[0]

    @pl.loop(0, count // 4)
    def _(n):
        for m in range(4):
            wait(4 * n + m)
        for m in range(4):
            multiply(4 * n + m)

    @pl.loop(count // 4 * 4, count)
    def _(n):
        wait(n)
        multiply(n)

    def out_copy(r):
        return pltpu.make_async_copy(
            accum.at[pl.ds(r * B, B)], out.at[pl.ds(r * B, B)], out_sems.at[r]
        )

    for r in range(TR):
        out_copy(r).start()

    def add(s, total):
        x = accum[pl.ds(pl.multiple_of(s * 32, 32), 32), :]
        return total + jnp.sum((x * x).reshape(4, 8, TC * B), axis=0)

    total = lax.fori_loop(0, TR * B // 32, add, jnp.zeros((8, TC * B), jnp.float32))
    sums[...] = jnp.sum(total, axis=0, keepdims=True)
    for r in range(TR):
        out_copy(r).wait()


def products(info, tables, first):
    return pl.pallas_call(
        product_kernel,
        out_shape=(
            jax.ShapeDtypeStruct((TR * B, TC * B), jnp.float32),
            jax.ShapeDtypeStruct((1, TC * B), jnp.float32),
        ),
        in_specs=[SMEM] * (1 + 2 * ROUNDS) + [ANY] * len(first),
        out_specs=(ANY, VMEM),
        scratch_shapes=[
            pltpu.VMEM((TR * B, TC * B), jnp.float32),
            pltpu.VMEM((C_BLOCKS, B, B), jnp.bfloat16),
            pltpu.VMEM((WINDOW * PANEL, B, TC * B), jnp.bfloat16),
            pltpu.SMEM((C_BLOCKS,), jnp.int32),
            pltpu.SMEM((C_BLOCKS,), jnp.int32),
            pltpu.SMEM((2,), jnp.int32),
            pltpu.SemaphoreType.DMA((C_BLOCKS + R_BLOCKS,)),
            pltpu.SemaphoreType.DMA((TR,)),
        ],
        compiler_params=pltpu.CompilerParams(vmem_limit_bytes=58 * 1024 * 1024),
        name="products",
    )(info, *tables, *first)


def scale_kernel(total, x, out, wide, tiles, in_sems, out_sems):
    def in_copy(r):
        return pltpu.make_async_copy(x.at[pl.ds(r * B, B)], wide.at[r], in_sems.at[r])

    def out_copy(r):
        return pltpu.make_async_copy(tiles.at[r], out.at[pl.ds(r * B, B)], out_sems.at[r])

    for r in range(TR):
        in_copy(r).start()
    factor = (TR * 8 * B) / (total[...] + EPS)
    for r in range(TR):
        in_copy(r).wait()

        @pl.loop(0, B // 32)
        def _(s, r=r):
            at = pl.ds(pl.multiple_of(s * 32, 32), 32)
            value = wide[r, at, :]
            tiles[r, at, :] = (value * value * factor).astype(jnp.bfloat16)

        out_copy(r).start()
    for r in range(TR):
        out_copy(r).wait()


def scale(total, expanded):
    return pl.pallas_call(
        scale_kernel,
        out_shape=jax.ShapeDtypeStruct((TR * B, TC * B), jnp.bfloat16),
        in_specs=[VMEM, ANY],
        out_specs=ANY,
        scratch_shapes=[
            pltpu.VMEM((TR, B, TC * B), jnp.float32),
            pltpu.VMEM((TR, B, TC * B), jnp.bfloat16),
            pltpu.SemaphoreType.DMA((TR,)),
            pltpu.SemaphoreType.DMA((TR,)),
        ],
        compiler_params=pltpu.CompilerParams(vmem_limit_bytes=58 * 1024 * 1024),
        name="scale",
    )(total, expanded)


def column_total(part):
    def turn(x, by):
        return lax.ppermute(x, "row", [(a, (a + 2 * by) % GRID_R) for a in range(GRID_R)])

    part = part + (turn(part, 1) + turn(part, 2) + turn(part, 3))
    return part + lax.ppermute(part, "row", [(a, a ^ 1) for a in range(GRID_R)])


def per_device(blocks, block_rows, block_cols, counts, sections):
    info = jnp.stack(
        [lax.axis_index("row"), lax.axis_index("col"), sections[0], sections[1], counts[0, 0]]
    ).astype(jnp.int32)
    args = (info, block_rows[0, 0], block_cols[0, 0], blocks[0, 0].reshape(CAP * B, B))
    first, tables, _ = send(PIECE, 0, "cr", *args)

    expanded, part = products(info, tables, first)
    return scale(column_total(part), expanded)


def solution(mesh):
    in_specs = (
        P("row", "col", None, None, None),
        P("row", "col", None),
        P("row", "col", None),
        P("row", "col"),
        P(),
    )
    out_specs = P("row", "col")
    return jax.shard_map(
        per_device, mesh=mesh, in_specs=in_specs, out_specs=out_specs, check_vma=False
    )
```
